1024 devices in a mesh: dp: 64 (over z, core), expert: 16 (over y, x).
Axes of the slice: x: 4, y: 4, z: 32, core: 2. Of those that a mesh axis runs over, the one named last changes fastest.
Arguments:
- tokens: bfloat16 [3072, 4096], P('dp', 'expert'), may hold values from -6 to 6
- picks: int32 [3072, 8], P('dp'), may hold values from 0 to 127, all different within a row; in each aligned block of 48 rows (0 to 47, 48 to 95, ...) at most 6 rows name the same one
- gates: float32 [3072, 8], P('dp'), may hold values from 0.05 to 0.5
- w_gate: bfloat16 [64, 4096, 1536], P('dp', 'expert'), may hold values from -0.09375 to 0.09375
- w_up: bfloat16 [64, 4096, 1536], P('dp', 'expert'), may hold values from -0.09375 to 0.09375
- w_down: bfloat16 [64, 1536, 4096], P('dp', None, 'expert'), may hold values from -0.15625 to 0.15625
- cotangent: bfloat16 [3072, 4096], P('dp', 'expert'), may hold values from -6 to 6
Outputs:
- mixed: bfloat16 [3072, 4096], P('dp', 'expert')
- grad_tokens: bfloat16 [3072, 4096], P('dp', 'expert')
- grad_gates: float32 [3072, 8], P('dp')
The draws below stay inside these ranges and needn't reach their ends.
Inputs may be any that keep to these rules, and one draw needn't show every extreme that they name: Among the 48 tokens of one index of dp, no expert is named by more than 6 picks, a bound that some block reaches; the 8 picks of a token differ.
All inputs are finite; a program needn't handle non-finite values.
Results may differ from the reference program's by a relative error of at most 0.0064.
Values may be sent and summed in bfloat16 or wider, within the bound.
No kernel may reach another device: no remote copies, remote signals or barrier semaphores. Data moves between devices by JAX's collectives and lax.ppermute only.
A program may use at most 64 MiB of HBM per device.

```python
import math
import jax
import jax.numpy as jnp
import numpy as np
from jax import lax

D = 4096
H = 1536
ROUTED = 128
TOP = 8
TOK_ROW = 48
CAP = 6
EXPERTS = 64
TOKENS = 3072
N_DP = 64


def levels(key, dims, shards, least, high):
    def one(dim, parts):
        draws = jax.random.uniform(jax.random.fold_in(jax.random.fold_in(key, 6), dim), (parts,), jnp.float32, least / len(shards), high / len(shards))
        return jnp.repeat(jnp.exp(draws), dims[dim] // parts).reshape((-1,) + (1,) * (len(dims) - dim - 1))

    level = one(*shards[0])
    for cut in shards[1:]:
        level = level * one(*cut)
    return level


def deal_out(rng, own, number, rows, count, top, bound, slope):
    ranking = jax.random.permutation(rng, count)
    heavy_load, ordinary = load_shares(count, rows * top, bound, slope, True), load_shares(count, rows * top, bound, slope, False)
    places = jnp.arange(count)

    def named(sizes, offset_by):
        used = int((sizes > 0).sum())
        fixed = max(1, used // 4)
        moved = fixed + (places - fixed + offset_by * (used - fixed)) % max(1, count - fixed)
        return jnp.zeros((count,), jnp.int32).at[ranking[jnp.where(places < fixed, places, moved)]].set(jnp.asarray(sizes, jnp.int32))

    sizes = jnp.where(number % 4 == 0, named(heavy_load, number // 4), named(ordinary, number - number // 4 - 1))
    mixed = jax.random.permutation(jax.random.fold_in(own, 3), count)
    source_of, taker = mixed[0:count // 2 * 2:2], mixed[1:count // 2 * 2:2]
    margin = jnp.minimum(sizes[source_of] - 1, bound - sizes[taker]) // 2
    margin = jnp.where((source_of == ranking[0]) | (taker == ranking[0]) | (sizes[taker] == 0), 0, jnp.maximum(margin, 0))
    moved = jax.random.randint(jax.random.fold_in(own, 4), (count // 2,), 0, 1 << 20) % (margin + 1)
    sizes = sizes.at[source_of].add(-moved).at[taker].add(moved)
    members = jnp.searchsorted(jnp.cumsum(sizes), jnp.arange(rows * top), side="right").astype(jnp.int32)
    grid = members.reshape(top, rows).T
    grid = grid[jax.random.permutation(jax.random.fold_in(own, 1), rows)]
    offset_by = jax.random.randint(jax.random.fold_in(own, 2), (rows, 1), 0, top)
    return jnp.take_along_axis(grid, (jnp.arange(top)[None, :] + offset_by) % top, axis=1)


def load_shares(count, total, reach, skew, full):
    loads = [(1 << 20) // math.isqrt(standing ** skew) + 1 for standing in range(1, count + 1)]
    largest = reach if full else min(reach, max(-(-total // count), total * loads[0] // sum(loads)))
    least = 1 if total - largest >= count - 1 else 0
    given, rest = [largest] + [least] * (count - 1), total - largest - least * (count - 1)
    while rest > 0:
        candidates = [i for i in range(1, count) if given[i] < largest] or [i for i in range(1, count) if given[i] < reach]
        whole, remaining = sum([loads[i] for i in candidates]), rest
        for i in candidates:
            addition = min(reach - given[i], max(1, remaining * loads[i] // whole), rest)
            given[i] = given[i] + addition
            rest = rest - addition
    return np.array(given)


def scatter_about(key, shape, scale, bound, cuts=(), held_as=jnp.bfloat16):
    entries = jax.random.normal(key, shape, jnp.float32) * scale
    if len(cuts) > 0:
        entries = levels(key, shape, cuts, -0.22, 0.18) * entries
    return jnp.clip(entries, min=-bound, max=bound).astype(held_as)


def setup_inputs(seed: int = 0) -> dict:
    key_of = jax.random.split(jax.random.key(seed), 8)
    tokens = scatter_about(key_of[0], (TOKENS, D), 1.0, 6.0, ((0, 64), (1, 16)))
    picks_keys = jax.random.split(jax.random.fold_in(key_of[1], 1), TOKENS // TOK_ROW)
    picks_turns = jax.random.permutation(jax.random.fold_in(key_of[1], 3), TOKENS // TOK_ROW)
    picks = jax.vmap(lambda own, number: deal_out(jax.random.fold_in(key_of[1], 2), own, number, TOK_ROW, ROUTED, TOP, CAP, 2))(picks_keys, picks_turns).reshape((TOKENS, TOP))
    gates = jnp.clip(jnp.exp(math.log(0.5) - 2.3025851 * jax.random.uniform(key_of[2], (TOKENS, TOP), jnp.float32) ** levels(key_of[2], (TOKENS, TOP), ((0, 64),), -0.2, 0.2)), 0.05, 0.5)
    w_gate = scatter_about(key_of[3], (EXPERTS, D, H), D ** -0.5, 0.09375, ((0, 64), (1, 16)))
    w_up = scatter_about(key_of[4], (EXPERTS, D, H), D ** -0.5, 0.09375, ((0, 64), (1, 16)))
    w_down = scatter_about(key_of[5], (EXPERTS, H, D), H ** -0.5, 0.15625, ((0, 64), (2, 16)))
    cotangent = scatter_about(key_of[6], (TOKENS, D), 1.0, 6.0, ((0, 64), (1, 16)))
    return dict(tokens=tokens, picks=picks, gates=gates, w_gate=w_gate, w_up=w_up, w_down=w_down, cotangent=cotangent)


def silu_parts(gate_pre):
    logistic = jax.nn.sigmoid(gate_pre)
    return gate_pre * logistic, logistic * (1.0 + gate_pre * (1.0 - logistic))


def expert_pass(inputs):
    tok_in, grad_in, gate_mat, up_mat, down_mat = inputs
    gate_pre = jnp.dot(tok_in, gate_mat, preferred_element_type=jnp.float32)
    up_pre = jnp.dot(tok_in, up_mat, preferred_element_type=jnp.float32)
    silu_val, silu_slope = silu_parts(gate_pre)
    hidden_act = (silu_val * up_pre).astype(jnp.bfloat16)
    expert_out = jnp.dot(hidden_act, down_mat, preferred_element_type=jnp.float32).astype(jnp.bfloat16)
    grad_hidden = jnp.dot(grad_in, down_mat.T, preferred_element_type=jnp.float32)
    grad_gate = (grad_hidden * up_pre * silu_slope).astype(jnp.bfloat16)
    grad_up = (grad_hidden * silu_val).astype(jnp.bfloat16)
    grad_pick = jnp.dot(grad_gate, gate_mat.T, preferred_element_type=jnp.float32)
    grad_pick = grad_pick + jnp.dot(grad_up, up_mat.T, preferred_element_type=jnp.float32)
    return expert_out, grad_pick.astype(jnp.bfloat16)


def reference(tokens, picks, gates, w_gate, w_up, w_down, cotangent):
    pair_count = TOK_ROW * TOP
    slot_total = N_DP * CAP
    row_picks = picks.reshape(N_DP, pair_count)
    onehot = (row_picks[:, :, None] == jnp.arange(ROUTED, dtype=jnp.int32)[None, None, :]).astype(jnp.int32)
    slot_rank = jnp.sum((jnp.cumsum(onehot, axis=1) - onehot) * onehot, axis=2)
    in_window = row_picks < EXPERTS
    row_ids = jnp.arange(N_DP, dtype=jnp.int32)[:, None]
    slot_index = (row_picks * N_DP + row_ids) * CAP + slot_rank
    limit = EXPERTS * slot_total
    slot_index = jnp.where(in_window, slot_index, limit).reshape(-1).astype(jnp.int32)
    token_id = (jnp.arange(TOKENS * TOP, dtype=jnp.int32) // TOP).astype(jnp.int32)
    pair_tok = tokens[token_id]
    pair_grad = (gates.reshape(-1, 1) * cotangent[token_id].astype(jnp.float32)).astype(jnp.bfloat16)
    tok_slots = jnp.zeros((limit, D), jnp.bfloat16).at[slot_index].set(pair_tok, mode="drop")
    grad_slots = jnp.zeros((limit, D), jnp.bfloat16).at[slot_index].set(pair_grad, mode="drop")
    outs, grads = lax.map(expert_pass, (tok_slots.reshape(EXPERTS, slot_total, D), grad_slots.reshape(EXPERTS, slot_total, D), w_gate, w_up, w_down))
    outs = outs.reshape(limit, D)
    grads = grads.reshape(limit, D)
    clipped = jnp.minimum(slot_index, limit - 1).astype(jnp.int32)
    live = in_window.reshape(-1, 1)
    pair_out = jnp.where(live, outs[clipped].astype(jnp.float32), 0.0).reshape(TOKENS, TOP, D)
    pair_dx = jnp.where(live, grads[clipped].astype(jnp.float32), 0.0).reshape(TOKENS, TOP, D)
    mixed = jnp.sum(gates[:, :, None] * pair_out, axis=1).astype(jnp.bfloat16)
    grad_tokens = jnp.sum(pair_dx, axis=1).astype(jnp.bfloat16)
    grad_gates = jnp.sum(cotangent.astype(jnp.float32)[:, None, :] * pair_out, axis=2)
    return mixed, grad_tokens, grad_gates
```

```python
import jax
import jax.numpy as jnp
from jax import lax
from jax.sharding import PartitionSpec as P

CAP = 6
LANES = 128
F32 = jnp.float32
BF16 = jnp.bfloat16


def split3(v):
    hi = v.astype(BF16).astype(F32)
    mid = (v - hi).astype(BF16).astype(F32)
    return hi, mid, v - hi - mid


def routing(picks, gates, experts):
    ids = jnp.arange(experts, dtype=jnp.int32)
    names = picks[:, :, None] == ids[None, None, :]
    member = jnp.any(names, axis=1)
    gate_te = jnp.sum(jnp.where(names, gates[:, :, None], 0.0), axis=1)
    rows = picks.shape[0]
    before = jnp.arange(rows)[:, None] > jnp.arange(rows)[None, :]
    rank = jnp.dot(before.astype(BF16), member.astype(BF16), preferred_element_type=F32)
    rank = jnp.where(member, rank, -1.0)
    return names, rank, gate_te


def shards(tokens, picks, gates, w_gate, w_up, w_down, cotangent):
    rows, feats = tokens.shape
    experts = lax.axis_size("dp")
    parts = lax.axis_size("expert")
    halves = feats // LANES
    slots = experts * CAP
    pieces = 2 * halves * CAP
    hidden = w_gate.shape[2]
    w_gate, w_up, w_down = w_gate[0], w_up[0], w_down[0]

    names, rank, gate_te = routing(picks, gates, experts)
    rank_t = rank.T
    gate_t = gate_te.T

    j = jnp.arange(pieces, dtype=jnp.int32)
    j_blk, j_slot = j // CAP, (j % CAP).astype(F32)
    c = jnp.arange(2 * halves * rows, dtype=jnp.int32)
    c_blk = c // rows
    rank_c = jnp.tile(rank_t, (1, 2 * halves))
    same = j_blk[:, None] == c_blk[None, :]
    pick_c = (rank_c[:, None, :] == j_slot[None, :, None]) & same[None]
    source = jnp.concatenate(
        [v[:, h * LANES : (h + 1) * LANES] for v in (tokens, cotangent) for h in range(halves)], axis=0
    )
    packed = jnp.dot(
        pick_c.astype(BF16).reshape(experts * pieces, -1), source, preferred_element_type=F32
    )
    hit = rank_t[:, None, :] == j_slot[None, :, None]
    scale = jnp.sum(jnp.where(hit, gate_t[:, None, :], 0.0), axis=2, keepdims=True)
    scale = jnp.where((j_blk >= halves)[None, :, None], scale, 1.0)
    packed = (packed.reshape(experts, pieces, LANES) * scale).astype(BF16)

    recv = lax.all_to_all(packed, "dp", split_axis=0, concat_axis=0, tiled=True)

    recv = recv.reshape(experts, 2, halves, CAP, LANES).transpose(1, 0, 3, 2, 4)
    recv = recv.reshape(2, slots, feats)
    tok, grad = recv[0], recv[1]
    pre = jnp.concatenate(
        [
            jnp.dot(tok, w_gate, preferred_element_type=F32).astype(BF16),
            jnp.dot(tok, w_up, preferred_element_type=F32).astype(BF16),
            lax.dot_general(grad, w_down, (((1,), (1,)), ((), ())), preferred_element_type=F32).astype(BF16),
        ],
        axis=1,
    )
    own = slots // parts
    pre = lax.all_to_all(
        pre.reshape(parts, own, 3 * hidden), "expert", split_axis=0, concat_axis=0, tiled=True
    )
    pre = jnp.sum(pre.astype(F32), axis=0)
    gate_pre, up_pre, grad_hidden = pre[:, :hidden], pre[:, hidden : 2 * hidden], pre[:, 2 * hidden :]
    logistic = jax.nn.sigmoid(gate_pre)
    silu = gate_pre * logistic
    act = (silu * up_pre).astype(BF16)
    grad_gate = (grad_hidden * up_pre * (logistic * (1.0 + gate_pre * (1.0 - logistic)))).astype(BF16)
    grad_up = (grad_hidden * silu).astype(BF16)
    dots = jnp.sum(act.astype(F32) * grad_hidden, axis=1, keepdims=True)
    dots_hi = dots.astype(BF16)
    dots_lo = (dots - dots_hi.astype(F32)).astype(BF16)
    lane = jnp.arange(LANES)[None, :]
    extra = jnp.where(lane == 0, dots_hi, jnp.where(lane == 1, dots_lo, jnp.zeros((), BF16)))
    every = lax.all_gather(
        jnp.concatenate([act, grad_gate, grad_up, extra], axis=1), "expert", axis=0, tiled=True
    )

    dots = every[:, 3 * hidden].astype(F32) + every[:, 3 * hidden + 1].astype(F32)
    dots = jnp.pad(dots.reshape(slots // LANES, LANES), ((0, 48 - slots // LANES), (0, 0)))
    dots = lax.all_gather(dots, "dp", axis=0, tiled=False)[:, : slots // LANES]

    expert_out = jnp.dot(every[:, :hidden], w_down, preferred_element_type=F32)
    grad_pick = lax.dot_general(
        every[:, hidden : 2 * hidden], w_gate, (((1,), (1,)), ((), ())), preferred_element_type=F32
    ) + lax.dot_general(
        every[:, 2 * hidden : 3 * hidden], w_up, (((1,), (1,)), ((), ())), preferred_element_type=F32
    )
    back = jnp.stack([expert_out.astype(BF16), grad_pick.astype(BF16)])
    back = back.reshape(2, experts, CAP, halves, LANES).transpose(1, 0, 3, 2, 4)
    back = lax.all_to_all(
        back.reshape(experts, pieces, LANES), "dp", split_axis=0, concat_axis=0, tiled=True
    )

    kinds = [g for g in split3(gate_t)] + [jnp.ones_like(gate_t)]
    value = jnp.concatenate([g for g in kinds for _ in range(halves)], axis=1)
    m = jnp.arange(4 * halves * rows, dtype=jnp.int32)
    m_kind, m_half = m // (halves * rows), m // rows % halves
    m_array = (m_kind == 3).astype(jnp.int32)
    meets = j_blk[:, None] == (m_array * halves + m_half)[None, :]
    rank_m = jnp.tile(rank_t, (1, 4 * halves))
    mix = jnp.where((rank_m[:, None, :] == j_slot[None, :, None]) & meets[None], value[:, None, :], 0.0)
    out = lax.dot_general(
        mix.astype(BF16).reshape(experts * pieces, -1),
        back.reshape(experts * pieces, LANES),
        (((0,), (0,)), ((), ())),
        preferred_element_type=F32,
    ).reshape(4, halves, rows, LANES)
    mixed = out[0] + out[1] + out[2]
    mixed = jnp.concatenate([mixed[h] for h in range(halves)], axis=1).astype(BF16)
    grad_tokens = jnp.concatenate([out[3, h] for h in range(halves)], axis=1).astype(BF16)

    me = lax.axis_index("dp")
    dots = lax.dynamic_slice_in_dim(dots.reshape(experts, slots), me * CAP, CAP, axis=1)
    dots_te = sum(jnp.where(rank_t == s, dots[:, s : s + 1], 0.0) for s in range(CAP)).T
    grad_gates = jnp.sum(jnp.where(names, dots_te[:, None, :], 0.0), axis=2) / gates
    return mixed, grad_tokens, grad_gates


def solution(mesh):
    placed = (
        P("dp", "expert"),
        P("dp", None),
        P("dp", None),
        P("dp", "expert", None),
        P("dp", "expert", None),
        P("dp", None, "expert"),
        P("dp", "expert"),
    )
    return jax.shard_map(
        shards,
        mesh=mesh,
        in_specs=placed,
        out_specs=(P("dp", "expert"), P("dp", "expert"), P("dp", None)),
        check_vma=False,
    )
```

```python
import jax
import jax.numpy as jnp
from jax import lax
from jax.sharding import Mesh, PartitionSpec as P

CAP = 6
LANES = 128
SIDE = 4
F32 = jnp.float32
BF16 = jnp.bfloat16


def split3(v):
    hi = v.astype(BF16).astype(F32)
    mid = (v - hi).astype(BF16).astype(F32)
    return hi, mid, v - hi - mid


def exchange(v, axes):
    return lax.all_to_all(v, axes, split_axis=0, concat_axis=0, tiled=True)


def routing(picks, gates, experts):
    ids = jnp.arange(experts, dtype=jnp.int32)
    names = picks[:, :, None] == ids[None, None, :]
    member = jnp.any(names, axis=1)
    gate_te = jnp.sum(jnp.where(names, gates[:, :, None], 0.0), axis=1)
    rows = picks.shape[0]
    before = jnp.arange(rows)[:, None] > jnp.arange(rows)[None, :]
    rank = jnp.dot(before.astype(BF16), member.astype(BF16), preferred_element_type=F32)
    rank = jnp.where(member, rank, -1.0)
    return names, rank, gate_te


def times(a, b):
    return jnp.dot(a, b, preferred_element_type=F32)


def times_t(a, b):
    return lax.dot_general(a, b, (((1,), (1,)), ((), ())), preferred_element_type=F32)


def shards(tokens, picks, gates, w_gate, w_up, w_down, cotangent):
    rows, feats = tokens.shape
    experts = lax.axis_size("dp")
    halves = feats // LANES
    pieces = 2 * halves * CAP
    hidden = w_gate.shape[2]
    quarter = experts // SIDE
    mine = quarter * CAP
    own = mine // SIDE
    all_gate, all_up, all_down = (lax.all_gather(w[0], "x", axis=0, tiled=False) for w in (w_gate, w_up, w_down))

    names, rank, gate_te = routing(picks, gates, experts)
    rank_t = rank.T
    gate_t = gate_te.T

    j = jnp.arange(pieces, dtype=jnp.int32)
    j_blk, j_slot = j // CAP, (j % CAP).astype(F32)
    c = jnp.arange(2 * halves * rows, dtype=jnp.int32)
    c_blk = c // rows
    rank_c = jnp.tile(rank_t, (1, 2 * halves))
    slot_c = rank_c[:, None, :] == j_slot[None, :, None]
    same = (j_blk[:, None] == c_blk[None, :])[None]
    other = (j_blk[:, None] + halves == c_blk[None, :])[None]
    source = jnp.concatenate(
        [v[:, h * LANES : (h + 1) * LANES] for v in (tokens, cotangent) for h in range(halves)], axis=0
    )

    def select(mask):
        mask = (slot_c & mask).astype(BF16).reshape(experts * pieces, -1)
        return times(mask, source).reshape(experts, pieces, LANES)

    hit = rank_t[:, None, :] == j_slot[None, :, None]
    scale = jnp.sum(jnp.where(hit, gate_t[:, None, :], 0.0), axis=2, keepdims=True)
    scale = jnp.where((j_blk >= halves)[None, :, None], scale, 1.0)
    packed = (select(same) * scale).astype(BF16)

    recv = exchange(packed, "dp")
    recv = exchange(recv.reshape(SIDE, quarter * pieces, LANES), "x")

    q = jnp.arange(quarter * pieces, dtype=jnp.int32)
    q_place = (q % pieces) // CAP * mine + q // pieces * CAP + q % CAP
    order = (q_place[None, :] == q[:, None]).astype(BF16)
    recv = lax.dot_general(order, recv, (((1,), (1,)), ((), ())), preferred_element_type=BF16)
    recv = recv.reshape(2, halves, mine, SIDE, LANES).transpose(0, 2, 3, 1, 4)
    recv = recv.reshape(2, mine, SIDE * feats)
    tok, grad = recv[0], recv[1]
    pre = [times(tok, w.reshape(SIDE * feats, hidden)).astype(BF16) for w in (all_gate, all_up)]
    pre.append(sum(times_t(grad[:, i * feats : (i + 1) * feats], all_down[i]) for i in range(SIDE)).astype(BF16))
    pre = jnp.concatenate(pre, axis=1)

    pre = exchange(pre.reshape(SIDE, own, 3 * hidden), "y")
    pre = jnp.sum(pre.astype(F32), axis=0)
    gate_pre, up_pre, grad_hidden = pre[:, :hidden], pre[:, hidden : 2 * hidden], pre[:, 2 * hidden :]
    logistic = jax.nn.sigmoid(gate_pre)
    silu = gate_pre * logistic
    act = (silu * up_pre).astype(BF16)
    grad_gate = (grad_hidden * up_pre * (logistic * (1.0 + gate_pre * (1.0 - logistic)))).astype(BF16)
    grad_up = (grad_hidden * silu).astype(BF16)
    every = lax.all_gather(jnp.concatenate([act, grad_gate, grad_up], axis=1), "y", axis=0, tiled=True)

    act, grad_gate, grad_up = every[:, :hidden], every[:, hidden : 2 * hidden], every[:, 2 * hidden :]
    expert_out = [times(act, all_down[i]).astype(BF16) for i in range(SIDE)]
    grad_pick = [
        (times_t(grad_gate, all_gate[i]) + times_t(grad_up, all_up[i])).astype(BF16) for i in range(SIDE)
    ]
    back = jnp.concatenate(
        [
            v[i][:, h * LANES : (h + 1) * LANES]
            for v in (expert_out, grad_pick)
            for h in range(halves)
            for i in range(SIDE)
        ],
        axis=0,
    ).reshape(2 * halves, SIDE, mine, LANES).transpose(1, 0, 2, 3).reshape(SIDE, quarter * pieces, LANES)
    back = jnp.stack(
        [
            lax.dot_general(order, back[i], (((0,), (0,)), ((), ())), preferred_element_type=BF16)
            for i in range(SIDE)
        ]
    )
    back = exchange(back, "x")
    back = exchange(back.reshape(experts, pieces, LANES), "dp")

    cot_rows = select(other)
    dots = jnp.sum(cot_rows * back.astype(F32), axis=2)
    dots = jnp.sum(dots.reshape(experts, 2 * halves, CAP)[:, :halves], axis=1)
    dots_te = sum(jnp.where(rank_t == s, dots[:, s : s + 1], 0.0) for s in range(CAP)).T
    local = jnp.sum(jnp.where(names, dots_te[:, None, :], 0.0), axis=2)
    parts = SIDE * SIDE
    local = jnp.broadcast_to(local.reshape(1, -1, LANES), (parts, local.size // LANES, LANES))
    grad_gates = jnp.sum(exchange(local, ("y", "x")), axis=0).reshape(gates.shape)

    kinds = [g for g in split3(gate_t)] + [jnp.ones_like(gate_t)]
    value = jnp.concatenate([g for g in kinds for _ in range(halves)], axis=1)
    m = jnp.arange(4 * halves * rows, dtype=jnp.int32)
    m_kind, m_half = m // (halves * rows), m // rows % halves
    m_array = (m_kind == 3).astype(jnp.int32)
    meets = j_blk[:, None] == (m_array * halves + m_half)[None, :]
    rank_m = jnp.tile(rank_t, (1, 4 * halves))
    mix = jnp.where((rank_m[:, None, :] == j_slot[None, :, None]) & meets[None], value[:, None, :], 0.0)
    out = lax.dot_general(
        mix.astype(BF16).reshape(experts * pieces, -1),
        back.reshape(experts * pieces, LANES),
        (((0,), (0,)), ((), ())),
        preferred_element_type=F32,
    ).reshape(4, halves, rows, LANES)
    mixed = out[0] + out[1] + out[2]
    mixed = jnp.concatenate([mixed[h] for h in range(halves)], axis=1).astype(BF16)
    grad_tokens = jnp.concatenate([out[3, h] for h in range(halves)], axis=1).astype(BF16)
    return mixed, grad_tokens, grad_gates


def solution(mesh):
    wide = Mesh(mesh.devices.reshape(mesh.devices.shape[0], SIDE, SIDE), ("dp", "y", "x"))
    split = ("y", "x")
    placed = (
        P("dp", split),
        P("dp", None),
        P("dp", None),
        P("dp", split, None),
        P("dp", split, None),
        P("dp", None, split),
        P("dp", split),
    )
    return jax.shard_map(
        shards,
        mesh=wide,
        in_specs=placed,
        out_specs=(P("dp", split), P("dp", split), P("dp", None)),
        check_vma=False,
    )
```

```python
import jax
import jax.numpy as jnp
from jax import lax
from jax.sharding import Mesh, PartitionSpec as P

CAP = 6
LANES = 128
SIDE = 4
F32 = jnp.float32
BF16 = jnp.bfloat16


def split3(v):
    hi = v.astype(BF16).astype(F32)
    mid = (v - hi).astype(BF16).astype(F32)
    return hi, mid, v - hi - mid


def exchange(v, axes):
    return lax.all_to_all(v, axes, split_axis=0, concat_axis=0, tiled=True)


def take(v, i):
    return lax.dynamic_index_in_dim(v, i % SIDE, axis=0, keepdims=False)


def routing(picks, gates, experts):
    ids = jnp.arange(experts, dtype=jnp.int32)
    names = picks[:, :, None] == ids[None, None, :]
    member = jnp.any(names, axis=1)
    gate_te = jnp.sum(jnp.where(names, gates[:, :, None], 0.0), axis=1)
    rows = picks.shape[0]
    before = jnp.arange(rows)[:, None] > jnp.arange(rows)[None, :]
    rank = jnp.dot(before.astype(BF16), member.astype(BF16), preferred_element_type=F32)
    rank = jnp.where(member, rank, -1.0)
    return names, rank, gate_te


def times(a, b):
    return jnp.dot(a, b, preferred_element_type=F32)


def times_t(a, b):
    return lax.dot_general(a, b, (((1,), (1,)), ((), ())), preferred_element_type=F32)


def shards(tokens, picks, gates, w_gate, w_up, w_down, cotangent):
    rows, feats = tokens.shape
    experts = lax.axis_size("dp")
    halves = feats // LANES
    pieces = 2 * halves * CAP
    hidden = w_gate.shape[2]
    quarter = experts // SIDE
    slots = experts * CAP
    block = quarter * CAP
    share = hidden // SIDE

    names, rank, gate_te = routing(picks, gates, experts)
    rank_t = rank.T
    gate_t = gate_te.T

    j = jnp.arange(pieces, dtype=jnp.int32)
    j_blk, j_slot = j // CAP, (j % CAP).astype(F32)
    c = jnp.arange(2 * halves * rows, dtype=jnp.int32)
    c_blk = c // rows
    rank_c = jnp.tile(rank_t, (1, 2 * halves))
    slot_c = rank_c[:, None, :] == j_slot[None, :, None]
    same = (j_blk[:, None] == c_blk[None, :])[None]
    other = (j_blk[:, None] + halves == c_blk[None, :])[None]
    source = jnp.concatenate(
        [v[:, h * LANES : (h + 1) * LANES] for v in (tokens, cotangent) for h in range(halves)], axis=0
    )

    def select(mask):
        mask = (slot_c & mask).astype(BF16).reshape(experts * pieces, -1)
        return times(mask, source).reshape(experts, pieces, LANES)

    hit = rank_t[:, None, :] == j_slot[None, :, None]
    scale = jnp.sum(jnp.where(hit, gate_t[:, None, :], 0.0), axis=2, keepdims=True)
    scale = jnp.where((j_blk >= halves)[None, :, None], scale, 1.0)
    packed = (select(same) * scale).astype(BF16)

    recv = exchange(packed, "dp")

    weights = jnp.concatenate([w_gate[0], w_up[0], w_down[0].T], axis=0)
    weights = jnp.stack([weights[:, i * share : (i + 1) * share] for i in range(SIDE)])
    me = lax.axis_index("x")
    weights = jnp.stack(
        [
            lax.ppermute(take(weights, me + i), "x", [(d, (d + i) % SIDE) for d in range(SIDE)])
            if i
            else take(weights, me)
            for i in range(SIDE)
        ]
    ).reshape(SIDE, 3, feats, share)

    q = jnp.arange(quarter * pieces, dtype=jnp.int32)
    q_place = (q % pieces) // CAP * block + q // pieces * CAP + q % CAP
    order = (q_place[None, :] == q[:, None]).astype(BF16)
    recv = recv.reshape(SIDE, quarter * pieces, LANES)
    recv = jnp.stack([jnp.dot(order, recv[i], preferred_element_type=BF16) for i in range(SIDE)])
    recv = recv.reshape(SIDE, 2 * halves, block, LANES)
    recv = jnp.concatenate([recv[:, i].reshape(slots, LANES) for i in range(2 * halves)], axis=1)
    recv, weights = lax.optimization_barrier((recv, weights))
    recv = exchange(jnp.broadcast_to(recv[None], (SIDE, slots, 2 * feats)), "x")
    recv = [take(recv, me + SIDE - i) for i in range(SIDE)]
    tok = jnp.concatenate([v[:, :feats] for v in recv], axis=1)
    grad = jnp.concatenate([v[:, feats:] for v in recv], axis=1)
    held = [weights[:, i].reshape(SIDE * feats, share) for i in range(3)]
    pre = [times(v, w).astype(BF16) for v, w in zip((tok, tok, grad), held)]
    pre = jnp.concatenate(pre, axis=1)

    pre = exchange(pre.reshape(SIDE, slots // SIDE, 3 * share), "y")
    pre = jnp.sum(pre.astype(F32), axis=0)
    gate_pre, up_pre, grad_hidden = pre[:, :share], pre[:, share : 2 * share], pre[:, 2 * share :]
    logistic = jax.nn.sigmoid(gate_pre)
    silu = gate_pre * logistic
    act = (silu * up_pre).astype(BF16)
    grad_gate = (grad_hidden * up_pre * (logistic * (1.0 + gate_pre * (1.0 - logistic)))).astype(BF16)
    grad_up = (grad_hidden * silu).astype(BF16)
    every = lax.all_gather(jnp.concatenate([act, grad_gate, grad_up], axis=1), "y", axis=0, tiled=True)

    act, grad_gate, grad_up = (every[:, i * share : (i + 1) * share] for i in range(3))
    expert_out = times_t(act, held[2]).astype(BF16)
    grad_pick = (times_t(grad_gate, held[0]) + times_t(grad_up, held[1])).astype(BF16)
    back = jnp.stack(
        [
            jnp.concatenate([v[:, i * feats : (i + 1) * feats] for v in (expert_out, grad_pick)], axis=1)
            for i in range(SIDE)
        ]
    )
    back = jnp.stack([take(back, me + SIDE - i) for i in range(SIDE)])
    back = jnp.sum(exchange(back, "x").astype(F32), axis=0).astype(BF16)
    back = jnp.stack(
        [back[:, i * LANES : (i + 1) * LANES].reshape(SIDE, block, LANES) for i in range(2 * halves)], axis=1
    ).reshape(SIDE, quarter * pieces, LANES)
    back = jnp.stack(
        [
            lax.dot_general(order, back[i], (((0,), (0,)), ((), ())), preferred_element_type=BF16)
            for i in range(SIDE)
        ]
    )
    back = exchange(back.reshape(experts, pieces, LANES), "dp")

    cot_rows = select(other)
    dots = jnp.sum(cot_rows * back.astype(F32), axis=2)
    dots = jnp.sum(dots.reshape(experts, 2 * halves, CAP)[:, :halves], axis=1)
    dots_te = sum(jnp.where(rank_t == s, dots[:, s : s + 1], 0.0) for s in range(CAP)).T
    local = jnp.sum(jnp.where(names, dots_te[:, None, :], 0.0), axis=2)
    parts = SIDE * SIDE
    local = jnp.broadcast_to(local.reshape(1, -1, LANES), (parts, local.size // LANES, LANES))
    grad_gates = jnp.sum(exchange(local, ("y", "x")), axis=0).reshape(gates.shape)

    kinds = [g for g in split3(gate_t)] + [jnp.ones_like(gate_t)]
    value = jnp.concatenate([g for g in kinds for _ in range(halves)], axis=1)
    m = jnp.arange(4 * halves * rows, dtype=jnp.int32)
    m_kind, m_half = m // (halves * rows), m // rows % halves
    m_array = (m_kind == 3).astype(jnp.int32)
    meets = j_blk[:, None] == (m_array * halves + m_half)[None, :]
    rank_m = jnp.tile(rank_t, (1, 4 * halves))
    mix = jnp.where((rank_m[:, None, :] == j_slot[None, :, None]) & meets[None], value[:, None, :], 0.0)
    out = lax.dot_general(
        mix.astype(BF16).reshape(experts * pieces, -1),
        back.reshape(experts * pieces, LANES),
        (((0,), (0,)), ((), ())),
        preferred_element_type=F32,
    ).reshape(4, halves, rows, LANES)
    mixed = out[0] + out[1] + out[2]
    mixed = jnp.concatenate([mixed[h] for h in range(halves)], axis=1).astype(BF16)
    grad_tokens = jnp.concatenate([out[3, h] for h in range(halves)], axis=1).astype(BF16)
    return mixed, grad_tokens, grad_gates


def solution(mesh):
    wide = Mesh(mesh.devices.reshape(mesh.devices.shape[0], SIDE, SIDE), ("dp", "y", "x"))
    split = ("y", "x")
    placed = (
        P("dp", split),
        P("dp", None),
        P("dp", None),
        P("dp", split, None),
        P("dp", split, None),
        P("dp", None, split),
        P("dp", split),
    )
    return jax.shard_map(
        shards,
        mesh=wide,
        in_specs=placed,
        out_specs=(P("dp", split), P("dp", split), P("dp", None)),
        check_vma=False,
    )
```

```python
import jax
import jax.numpy as jnp
from jax import lax
from jax.sharding import Mesh, PartitionSpec as P

CAP = 6
LANES = 128
SIDE = 4
F32 = jnp.float32
BF16 = jnp.bfloat16


def split3(v):
    hi = v.astype(BF16).astype(F32)
    mid = (v - hi).astype(BF16).astype(F32)
    return hi, mid, v - hi - mid


def exchange(v, axes):
    return lax.all_to_all(v, axes, split_axis=0, concat_axis=0, tiled=True)


def take(v, i):
    return lax.dynamic_index_in_dim(v, i % SIDE, axis=0, keepdims=False)


def routing(picks, gates, experts):
    ids = jnp.arange(experts, dtype=jnp.int32)
    names = picks[:, :, None] == ids[None, None, :]
    member = jnp.any(names, axis=1)
    gate_te = jnp.sum(jnp.where(names, gates[:, :, None], 0.0), axis=1)
    rows = picks.shape[0]
    before = jnp.arange(rows)[:, None] > jnp.arange(rows)[None, :]
    rank = jnp.dot(before.astype(BF16), member.astype(BF16), preferred_element_type=F32)
    rank = jnp.where(member, rank, -1.0)
    return names, rank, gate_te


def times(a, b):
    return jnp.dot(a, b, preferred_element_type=F32)


def times_t(a, b):
    return lax.dot_general(a, b, (((1,), (1,)), ((), ())), preferred_element_type=F32)


def shards(tokens, picks, gates, w_gate, w_up, w_down, cotangent):
    rows, feats = tokens.shape
    experts = lax.axis_size("dp")
    halves = feats // LANES
    pieces = 2 * halves * CAP
    hidden = w_gate.shape[2]
    quarter = experts // SIDE
    slots = experts * CAP
    block = quarter * CAP
    share = hidden // SIDE

    names, rank, gate_te = routing(picks, gates, experts)
    rank_t = rank.T
    gate_t = gate_te.T

    j = jnp.arange(pieces, dtype=jnp.int32)
    j_blk, j_slot = j // CAP, (j % CAP).astype(F32)
    c = jnp.arange(2 * halves * rows, dtype=jnp.int32)
    c_blk = c // rows
    rank_c = jnp.tile(rank_t, (1, 2 * halves))
    slot_c = rank_c[:, None, :] == j_slot[None, :, None]
    same = (j_blk[:, None] == c_blk[None, :])[None]
    other = (j_blk[:, None] + halves == c_blk[None, :])[None]
    source = jnp.concatenate(
        [v[:, h * LANES : (h + 1) * LANES] for v in (tokens, cotangent) for h in range(halves)], axis=0
    )

    def select(mask):
        mask = (slot_c & mask).astype(BF16).reshape(experts * pieces, -1)
        return times(mask, source).reshape(experts, pieces, LANES)

    hit = rank_t[:, None, :] == j_slot[None, :, None]
    scale = jnp.sum(jnp.where(hit, gate_t[:, None, :], 0.0), axis=2, keepdims=True)
    scale = jnp.where((j_blk >= halves)[None, :, None], scale, 1.0)
    packed = (select(same) * scale).astype(BF16)

    recv = exchange(packed, "dp")

    weights = jnp.concatenate([w_gate[0], w_up[0], w_down[0].T], axis=0)
    weights = jnp.stack([weights[:, i * share : (i + 1) * share] for i in range(SIDE)])
    me = lax.axis_index("x")
    weights = jnp.stack(
        [
            lax.ppermute(take(weights, me + i), "x", [(d, (d + i) % SIDE) for d in range(SIDE)])
            if i
            else take(weights, me)
            for i in range(SIDE)
        ]
    )
    weights = [take(weights, me + SIDE - i) for i in range(SIDE)]
    held = [jnp.concatenate([w[i * feats : (i + 1) * feats] for w in weights], axis=0) for i in range(3)]
    recv, *held = lax.optimization_barrier((recv, *held))

    q = jnp.arange(quarter * pieces, dtype=jnp.int32)
    q_place = (q % pieces) // CAP * block + q // pieces * CAP + q % CAP
    order = (q_place[None, :] == q[:, None]).astype(BF16)
    recv = recv.reshape(SIDE, quarter * pieces, LANES)
    recv = jnp.stack([jnp.dot(order, recv[i], preferred_element_type=BF16) for i in range(SIDE)])
    recv = recv.reshape(SIDE, 2 * halves, block, LANES)
    recv = jnp.concatenate([recv[:, i].reshape(slots, LANES) for i in range(2 * halves)], axis=1)
    recv = exchange(jnp.broadcast_to(recv[None], (SIDE, slots, 2 * feats)), "x")
    tok = jnp.concatenate([recv[i, :, :feats] for i in range(SIDE)], axis=1)
    grad = jnp.concatenate([recv[i, :, feats:] for i in range(SIDE)], axis=1)
    pre = [times(v, w).astype(BF16) for v, w in zip((tok, tok, grad), held)]
    pre = jnp.concatenate(pre, axis=1)

    pre = exchange(pre.reshape(SIDE, slots // SIDE, 3 * share), "y")
    pre = jnp.sum(pre.astype(F32), axis=0)
    gate_pre, up_pre, grad_hidden = pre[:, :share], pre[:, share : 2 * share], pre[:, 2 * share :]
    logistic = jax.nn.sigmoid(gate_pre)
    silu = gate_pre * logistic
    act = (silu * up_pre).astype(BF16)
    grad_gate = (grad_hidden * up_pre * (logistic * (1.0 + gate_pre * (1.0 - logistic)))).astype(BF16)
    grad_up = (grad_hidden * silu).astype(BF16)
    every = lax.all_gather(jnp.concatenate([act, grad_gate, grad_up], axis=1), "y", axis=0, tiled=True)

    act, grad_gate, grad_up = (every[:, i * share : (i + 1) * share] for i in range(3))
    expert_out = times_t(act, held[2]).astype(BF16)
    grad_pick = (times_t(grad_gate, held[0]) + times_t(grad_up, held[1])).astype(BF16)
    back = jnp.stack(
        [
            jnp.concatenate([v[:, i * feats : (i + 1) * feats] for v in (expert_out, grad_pick)], axis=1)
            for i in range(SIDE)
        ]
    )
    back = jnp.sum(exchange(back, "x").astype(F32), axis=0).astype(BF16)
    back = jnp.stack(
        [back[:, i * LANES : (i + 1) * LANES].reshape(SIDE, block, LANES) for i in range(2 * halves)], axis=1
    ).reshape(SIDE, quarter * pieces, LANES)
    back = jnp.stack(
        [
            lax.dot_general(order, back[i], (((0,), (0,)), ((), ())), preferred_element_type=BF16)
            for i in range(SIDE)
        ]
    )
    back = exchange(back.reshape(experts, pieces, LANES), "dp")

    cot_rows = select(other)
    dots = jnp.sum(cot_rows * back.astype(F32), axis=2)
    dots = jnp.sum(dots.reshape(experts, 2 * halves, CAP)[:, :halves], axis=1)
    dots_te = sum(jnp.where(rank_t == s, dots[:, s : s + 1], 0.0) for s in range(CAP)).T
    local = jnp.sum(jnp.where(names, dots_te[:, None, :], 0.0), axis=2)
    parts = SIDE * SIDE
    back, local = lax.optimization_barrier((back, local))
    local = jnp.broadcast_to(local.reshape(1, -1, LANES), (parts, local.size // LANES, LANES))
    grad_gates = jnp.sum(exchange(local, ("y", "x")), axis=0).reshape(gates.shape)

    kinds = [g for g in split3(gate_t)] + [jnp.ones_like(gate_t)]
    value = jnp.concatenate([g for g in kinds for _ in range(halves)], axis=1)
    m = jnp.arange(4 * halves * rows, dtype=jnp.int32)
    m_kind, m_half = m // (halves * rows), m // rows % halves
    m_array = (m_kind == 3).astype(jnp.int32)
    meets = j_blk[:, None] == (m_array * halves + m_half)[None, :]
    rank_m = jnp.tile(rank_t, (1, 4 * halves))
    mix = jnp.where((rank_m[:, None, :] == j_slot[None, :, None]) & meets[None], value[:, None, :], 0.0)
    out = lax.dot_general(
        mix.astype(BF16).reshape(experts * pieces, -1),
        back.reshape(experts * pieces, LANES),
        (((0,), (0,)), ((), ())),
        preferred_element_type=F32,
    ).reshape(4, halves, rows, LANES)
    mixed = out[0] + out[1] + out[2]
    mixed = jnp.concatenate([mixed[h] for h in range(halves)], axis=1).astype(BF16)
    grad_tokens = jnp.concatenate([out[3, h] for h in range(halves)], axis=1).astype(BF16)
    return mixed, grad_tokens, grad_gates


def solution(mesh):
    wide = Mesh(mesh.devices.reshape(mesh.devices.shape[0], SIDE, SIDE), ("dp", "y", "x"))
    split = ("y", "x")
    placed = (
        P("dp", split),
        P("dp", None),
        P("dp", None),
        P("dp", split, None),
        P("dp", split, None),
        P("dp", None, split),
        P("dp", split),
    )
    return jax.shard_map(
        shards,
        mesh=wide,
        in_specs=placed,
        out_specs=(P("dp", split), P("dp", split), P("dp", None)),
        check_vma=False,
    )
```

```python
import jax
import jax.numpy as jnp
from jax import lax
from jax.sharding import Mesh, PartitionSpec as P

CAP = 6
LANES = 128
SIDE = 4
F32 = jnp.float32
BF16 = jnp.bfloat16


def split3(v):
    hi = v.astype(BF16).astype(F32)
    mid = (v - hi).astype(BF16).astype(F32)
    return hi, mid, v - hi - mid


def exchange(v, axes):
    return lax.all_to_all(v, axes, split_axis=0, concat_axis=0, tiled=True)


def take(v, i):
    return lax.dynamic_index_in_dim(v, i % SIDE, axis=0, keepdims=False)


def routing(picks_t, gates_t, experts):
    ids = jnp.arange(experts, dtype=jnp.int32)
    names = picks_t[:, None, :] == ids[None, :, None]
    member = jnp.any(names, axis=0)
    gate = jnp.sum(jnp.where(names, gates_t[:, None, :], 0.0), axis=0)
    rows = picks_t.shape[1]
    before = jnp.arange(rows)[:, None] < jnp.arange(rows)[None, :]
    rank = jnp.dot(member.astype(BF16), before.astype(BF16), preferred_element_type=F32)
    return names, jnp.where(member, rank, -1000.0), gate


def times(a, b):
    return jnp.dot(a, b, preferred_element_type=F32)


def times_t(a, b):
    return lax.dot_general(a, b, (((1,), (1,)), ((), ())), preferred_element_type=F32)


def shards(tokens, picks, gates, w_gate, w_up, w_down, cotangent):
    rows, feats = tokens.shape
    experts = lax.axis_size("dp")
    halves = feats // LANES
    pieces = 2 * halves * CAP
    hidden = w_gate.shape[2]
    quarter = experts // SIDE
    slots = experts * CAP
    block = quarter * CAP
    share = hidden // SIDE

    names, rank, gate = routing(picks.T, gates.T, experts)

    j = jnp.arange(pieces, dtype=jnp.int32)
    j_row = j.astype(F32)[None, :, None]

    def rows_of(rank, blocks):
        return jnp.concatenate([rank + CAP * i for i in blocks], axis=1)[:, None, :]

    source = jnp.concatenate(
        [v[:, h * LANES : (h + 1) * LANES] for v in (tokens, cotangent) for h in range(halves)], axis=0
    )

    def select(target, rows_from):
        mask = (target == j_row).astype(BF16).reshape(experts * pieces, -1)
        return times(mask, rows_from).reshape(experts, pieces, LANES)

    hit = rank[:, None, :] == (j % CAP).astype(F32)[None, :, None]
    scale = jnp.sum(jnp.where(hit, gate[:, None, :], 0.0), axis=2, keepdims=True)
    scale = jnp.where((j >= halves * CAP)[None, :, None], scale, 1.0)
    packed = (select(rows_of(rank, range(2 * halves)), source) * scale).astype(BF16)

    recv = exchange(packed, "dp")

    weights = jnp.concatenate([w_gate[0], w_up[0], w_down[0].T], axis=0)
    weights = jnp.stack([weights[:, i * share : (i + 1) * share] for i in range(SIDE)])
    me = lax.axis_index("x")
    weights = jnp.stack(
        [
            lax.ppermute(take(weights, me + i), "x", [(d, (d + i) % SIDE) for d in range(SIDE)])
            if i
            else take(weights, me)
            for i in range(SIDE)
        ]
    )
    weights = [take(weights, me + SIDE - i) for i in range(SIDE)]
    held = [jnp.concatenate([w[i * feats : (i + 1) * feats] for w in weights], axis=0) for i in range(3)]
    recv, *held = lax.optimization_barrier((recv, *held))

    q = jnp.arange(quarter * pieces, dtype=jnp.int32)
    q_place = (q % pieces) // CAP * block + q // pieces * CAP + q % CAP
    order = (q_place[None, :] == q[:, None]).astype(BF16)
    recv = recv.reshape(SIDE, quarter * pieces, LANES)
    recv = lax.dot_general(order, recv, (((1,), (1,)), ((), ())), preferred_element_type=BF16)
    recv = recv.reshape(2 * halves, block, SIDE, LANES).transpose(2, 1, 0, 3).reshape(slots, 2 * feats)
    recv = exchange(jnp.broadcast_to(recv[None], (SIDE, slots, 2 * feats)), "x")
    tok = jnp.concatenate([recv[i, :, :feats] for i in range(SIDE)], axis=1)
    grad = jnp.concatenate([recv[i, :, feats:] for i in range(SIDE)], axis=1)
    pre = [times(v, w).astype(BF16) for v, w in zip((tok, tok, grad), held)]
    pre = jnp.concatenate(pre, axis=1)

    pre = exchange(pre.reshape(SIDE, slots // SIDE, 3 * share), "y")
    pre = jnp.sum(pre.astype(F32), axis=0)
    gate_pre, up_pre, grad_hidden = pre[:, :share], pre[:, share : 2 * share], pre[:, 2 * share :]
    logistic = jax.nn.sigmoid(gate_pre)
    silu = gate_pre * logistic
    act = (silu * up_pre).astype(BF16)
    grad_gate = (grad_hidden * up_pre * (logistic * (1.0 + gate_pre * (1.0 - logistic)))).astype(BF16)
    grad_up = (grad_hidden * silu).astype(BF16)
    every = lax.all_gather(jnp.concatenate([act, grad_gate, grad_up], axis=1), "y", axis=0, tiled=True)

    act, grad_gate, grad_up = (every[:, i * share : (i + 1) * share] for i in range(3))
    expert_out = times_t(act, held[2]).astype(BF16)
    grad_pick = (times_t(grad_gate, held[0]) + times_t(grad_up, held[1])).astype(BF16)
    back = jnp.stack(
        [
            jnp.concatenate([v[:, i * feats : (i + 1) * feats] for v in (expert_out, grad_pick)], axis=1)
            for i in range(SIDE)
        ]
    )
    back = jnp.sum(exchange(back, "x").astype(F32), axis=0).astype(BF16)
    back = back.reshape(SIDE, block, 2 * halves, LANES).transpose(2, 1, 0, 3)
    back = back.reshape(quarter * pieces, SIDE, LANES)
    back = lax.dot_general(order, back, (((0,), (0,)), ((), ())), preferred_element_type=BF16)
    back = back.transpose(1, 0, 2)
    back, rank, gate = lax.optimization_barrier((back, rank, gate))
    back = exchange(back.reshape(experts, pieces, LANES), "dp")

    cot_rows = select(rows_of(rank, range(halves)), source[halves * rows :]).astype(BF16)
    kinds = [g for g in split3(gate)] + [jnp.ones_like(gate)]
    value = jnp.concatenate([g for g in kinds for _ in range(halves)], axis=1)[:, None, :]
    mix = rows_of(rank, [i // 3 * halves + h for i in range(4) for h in range(halves)])
    mix = jnp.where(mix == j_row, value, 0.0).astype(BF16).reshape(experts * pieces, -1)
    back, cot_rows, mix = lax.optimization_barrier((back, cot_rows, mix))

    dots = jnp.sum(cot_rows.astype(F32) * back.astype(F32), axis=2)
    dots = sum(dots[:, h * CAP : (h + 1) * CAP] for h in range(halves))
    dots = sum(jnp.where(rank == i, dots[:, i : i + 1], 0.0) for i in range(CAP))
    local = jnp.sum(jnp.where(names, dots[None], 0.0), axis=1)
    back, local = lax.optimization_barrier((back, local))
    grad_gates = jnp.sum(exchange(jnp.broadcast_to(local, (SIDE * SIDE, *local.shape)), ("y", "x")), axis=0).T

    out = lax.dot_general(
        mix, back.reshape(experts * pieces, LANES), (((0,), (0,)), ((), ())), preferred_element_type=F32
    ).reshape(4, halves, rows, LANES)
    mixed = out[0] + out[1] + out[2]
    mixed = jnp.concatenate([mixed[h] for h in range(halves)], axis=1).astype(BF16)
    grad_tokens = jnp.concatenate([out[3, h] for h in range(halves)], axis=1).astype(BF16)
    return mixed, grad_tokens, grad_gates


def solution(mesh):
    wide = Mesh(mesh.devices.reshape(mesh.devices.shape[0], SIDE, SIDE), ("dp", "y", "x"))
    split = ("y", "x")
    placed = (
        P("dp", split),
        P("dp", None),
        P("dp", None),
        P("dp", split, None),
        P("dp", split, None),
        P("dp", None, split),
        P("dp", split),
    )
    return jax.shard_map(
        shards,
        mesh=wide,
        in_specs=placed,
        out_specs=(P("dp", split), P("dp", split), P("dp", None)),
        check_vma=False,
    )
```

```python
import jax
import jax.numpy as jnp
from jax import lax
from jax.sharding import Mesh, PartitionSpec as P

CAP = 6
LANES = 128
SIDE = 4
F32 = jnp.float32
BF16 = jnp.bfloat16


def split3(v):
    hi = v.astype(BF16).astype(F32)
    mid = (v - hi).astype(BF16).astype(F32)
    return hi, mid, v - hi - mid


def exchange(v, axes):
    return lax.all_to_all(v, axes, split_axis=0, concat_axis=0, tiled=True)


def take(v, i):
    return lax.dynamic_index_in_dim(v, i % SIDE, axis=0, keepdims=False)


def routing(picks_t, gates_t, experts):
    ids = jnp.arange(experts, dtype=jnp.int32)
    names = picks_t[:, None, :] == ids[None, :, None]
    member = jnp.any(names, axis=0)
    gate = jnp.sum(jnp.where(names, gates_t[:, None, :], 0.0), axis=0)
    rows = picks_t.shape[1]
    before = jnp.arange(rows)[:, None] < jnp.arange(rows)[None, :]
    rank = jnp.dot(member.astype(BF16), before.astype(BF16), preferred_element_type=F32)
    return names, jnp.where(member, rank, -1000.0), gate


def times(a, b):
    return jnp.dot(a, b, preferred_element_type=F32)


def times_t(a, b):
    return lax.dot_general(a, b, (((1,), (1,)), ((), ())), preferred_element_type=F32)


def shards(tokens, picks, gates, w_gate, w_up, w_down, cotangent):
    rows, feats = tokens.shape
    experts = lax.axis_size("dp")
    halves = feats // LANES
    pieces = 2 * halves * CAP
    hidden = w_gate.shape[2]
    quarter = experts // SIDE
    slots = experts * CAP
    block = quarter * CAP
    share = hidden // SIDE

    names, rank, gate = routing(picks.T, gates.T, experts)

    j = jnp.arange(pieces, dtype=jnp.int32)
    j_row = j.astype(F32)[None, :, None]

    def rows_of(rank, blocks):
        return jnp.concatenate([rank + CAP * i for i in blocks], axis=1)[:, None, :]

    source = jnp.concatenate(
        [v[:, h * LANES : (h + 1) * LANES] for v in (tokens, cotangent) for h in range(halves)], axis=0
    )

    def select(target, rows_from):
        mask = (target == j_row).astype(BF16).reshape(experts * pieces, -1)
        return times(mask, rows_from).reshape(experts, pieces, LANES)

    hit = rank[:, None, :] == (j % CAP).astype(F32)[None, :, None]
    scale = jnp.sum(jnp.where(hit, gate[:, None, :], 0.0), axis=2, keepdims=True)
    scale = jnp.where((j >= halves * CAP)[None, :, None], scale, 1.0)
    packed = (select(rows_of(rank, range(2 * halves)), source) * scale).astype(BF16)

    recv = exchange(packed, "dp")

    weights = jnp.concatenate([w_gate[0], w_up[0], w_down[0].T], axis=0)
    weights = jnp.stack([weights[:, i * share : (i + 1) * share] for i in range(SIDE)])
    me = lax.axis_index("x")
    weights = jnp.stack(
        [
            lax.ppermute(take(weights, me + i), "x", [(d, (d + i) % SIDE) for d in range(SIDE)])
            if i
            else take(weights, me)
            for i in range(SIDE)
        ]
    )
    weights = [take(weights, me + SIDE - i) for i in range(SIDE)]
    held = [jnp.concatenate([w[i * feats : (i + 1) * feats] for w in weights], axis=0) for i in range(3)]

    q = jnp.arange(quarter * pieces, dtype=jnp.int32)
    q_place = (q % pieces) // CAP * block + q // pieces * CAP + q % CAP
    order = (q_place[None, :] == q[:, None]).astype(BF16)
    recv = recv.reshape(SIDE, quarter * pieces, LANES)
    recv = lax.dot_general(order, recv, (((1,), (1,)), ((), ())), preferred_element_type=BF16)
    recv = recv.reshape(2 * halves, block, SIDE, LANES).transpose(2, 1, 0, 3).reshape(slots, 2 * feats)
    recv, *held = lax.optimization_barrier((recv, *held))
    recv = exchange(jnp.broadcast_to(recv[None], (SIDE, slots, 2 * feats)), "x")
    tok = jnp.concatenate([recv[i, :, :feats] for i in range(SIDE)], axis=1)
    grad = jnp.concatenate([recv[i, :, feats:] for i in range(SIDE)], axis=1)
    pre = [times(v, w).astype(BF16) for v, w in zip((tok, tok, grad), held)]
    pre = jnp.concatenate(pre, axis=1)

    pre = exchange(pre.reshape(SIDE, slots // SIDE, 3 * share), "y")
    pre = jnp.sum(pre.astype(F32), axis=0)
    gate_pre, up_pre, grad_hidden = pre[:, :share], pre[:, share : 2 * share], pre[:, 2 * share :]
    logistic = jax.nn.sigmoid(gate_pre)
    silu = gate_pre * logistic
    act = (silu * up_pre).astype(BF16)
    grad_gate = (grad_hidden * up_pre * (logistic * (1.0 + gate_pre * (1.0 - logistic)))).astype(BF16)
    grad_up = (grad_hidden * silu).astype(BF16)
    every = lax.all_gather(jnp.concatenate([act, grad_gate, grad_up], axis=1), "y", axis=0, tiled=True)

    act, grad_gate, grad_up = (every[:, i * share : (i + 1) * share] for i in range(3))
    expert_out = times_t(act, held[2]).astype(BF16)
    grad_pick = (times_t(grad_gate, held[0]) + times_t(grad_up, held[1])).astype(BF16)
    back = jnp.stack(
        [
            jnp.concatenate([v[:, i * feats : (i + 1) * feats] for v in (expert_out, grad_pick)], axis=1)
            for i in range(SIDE)
        ]
    )
    back = jnp.sum(exchange(back, "x").astype(F32), axis=0).astype(BF16)
    back = back.reshape(SIDE, block, 2 * halves, LANES).transpose(2, 1, 0, 3)
    back = back.reshape(quarter * pieces, SIDE, LANES)
    back = lax.dot_general(order, back, (((0,), (0,)), ((), ())), preferred_element_type=BF16)
    back = back.transpose(1, 0, 2)
    back, rank, gate = lax.optimization_barrier((back, rank, gate))
    back = exchange(back.reshape(experts, pieces, LANES), "dp")

    cot_rows = select(rows_of(rank, range(halves)), source[halves * rows :]).astype(BF16)
    kinds = [g for g in split3(gate)] + [jnp.ones_like(gate)]
    value = jnp.concatenate([g for g in kinds for _ in range(halves)], axis=1)[:, None, :]
    mix = rows_of(rank, [i // 3 * halves + h for i in range(4) for h in range(halves)])
    mix = jnp.where(mix == j_row, value, 0.0).astype(BF16).reshape(experts * pieces, -1)
    back, cot_rows, mix = lax.optimization_barrier((back, cot_rows, mix))

    dots = jnp.sum(cot_rows.astype(F32) * back.astype(F32), axis=2)
    dots = sum(dots[:, h * CAP : (h + 1) * CAP] for h in range(halves))
    dots = sum(jnp.where(rank == i, dots[:, i : i + 1], 0.0) for i in range(CAP))
    local = jnp.sum(jnp.where(names, dots[None], 0.0), axis=1)
    local = jnp.pad(local, ((0, 0), (0, LANES - rows)))
    back, local = lax.optimization_barrier((back, local))
    local = jnp.broadcast_to(local[None], (SIDE * SIDE, *local.shape))
    grad_gates = jnp.sum(exchange(local, ("y", "x")), axis=0)[:, :rows].T

    out = lax.dot_general(
        mix, back.reshape(experts * pieces, LANES), (((0,), (0,)), ((), ())), preferred_element_type=F32
    ).reshape(4, halves, rows, LANES)
    mixed = out[0] + out[1] + out[2]
    mixed = jnp.concatenate([mixed[h] for h in range(halves)], axis=1).astype(BF16)
    grad_tokens = jnp.concatenate([out[3, h] for h in range(halves)], axis=1).astype(BF16)
    return mixed, grad_tokens, grad_gates


def solution(mesh):
    wide = Mesh(mesh.devices.reshape(mesh.devices.shape[0], SIDE, SIDE), ("dp", "y", "x"))
    split = ("y", "x")
    placed = (
        P("dp", split),
        P("dp", None),
        P("dp", None),
        P("dp", split, None),
        P("dp", split, None),
        P("dp", None, split),
        P("dp", split),
    )
    return jax.shard_map(
        shards,
        mesh=wide,
        in_specs=placed,
        out_specs=(P("dp", split), P("dp", split), P("dp", None)),
        check_vma=False,
    )
```

```python
import jax
import jax.numpy as jnp
from jax import lax
from jax.sharding import Mesh, PartitionSpec as P

CAP = 6
LANES = 128
SIDE = 4
F32 = jnp.float32
BF16 = jnp.bfloat16


def split3(v):
    hi = v.astype(BF16).astype(F32)
    mid = (v - hi).astype(BF16).astype(F32)
    return hi, mid, v - hi - mid


def exchange(v, axes):
    return lax.all_to_all(v, axes, split_axis=0, concat_axis=0, tiled=True)


def take(v, i):
    return lax.dynamic_index_in_dim(v, i % SIDE, axis=0, keepdims=False)


def routing(picks_t, gates_t, experts):
    ids = jnp.arange(experts, dtype=jnp.int32)
    names = picks_t[:, None, :] == ids[None, :, None]
    member = jnp.any(names, axis=0)
    gate = jnp.sum(jnp.where(names, gates_t[:, None, :], 0.0), axis=0)
    rows = picks_t.shape[1]
    before = jnp.arange(rows)[:, None] < jnp.arange(rows)[None, :]
    rank = jnp.dot(member.astype(BF16), before.astype(BF16), preferred_element_type=F32)
    return names, jnp.where(member, rank, -1000.0), gate


def split2(v):
    hi = v.astype(BF16)
    return hi, (v - hi.astype(F32)).astype(BF16)


def times(a, b):
    return jnp.dot(a, b, preferred_element_type=F32)


def times_t(a, b):
    return lax.dot_general(a, b, (((1,), (1,)), ((), ())), preferred_element_type=F32)


def shards(tokens, picks, gates, w_gate, w_up, w_down, cotangent):
    rows, feats = tokens.shape
    experts = lax.axis_size("dp")
    halves = feats // LANES
    pieces = 2 * halves * CAP
    hidden = w_gate.shape[2]
    quarter = experts // SIDE
    slots = experts * CAP
    block = quarter * CAP
    share = hidden // SIDE

    names, rank, gate = routing(picks.T, gates.T, experts)

    j = jnp.arange(pieces, dtype=jnp.int32)
    j_row = j.astype(F32)[None, :, None]

    def rows_of(rank, blocks):
        return jnp.concatenate([rank + CAP * i for i in blocks], axis=1)[:, None, :]

    source = jnp.concatenate(
        [v[:, h * LANES : (h + 1) * LANES] for v in (tokens, cotangent) for h in range(halves)], axis=0
    )

    def select(target, rows_from):
        mask = (target == j_row).astype(BF16).reshape(experts * pieces, -1)
        return times(mask, rows_from).reshape(experts, pieces, LANES)

    hit = rank[:, None, :] == (j % CAP).astype(F32)[None, :, None]
    scale = jnp.sum(jnp.where(hit, gate[:, None, :], 0.0), axis=2, keepdims=True)
    scale = jnp.where((j >= halves * CAP)[None, :, None], scale, 1.0)
    packed = (select(rows_of(rank, range(2 * halves)), source) * scale).astype(BF16)

    recv = exchange(packed, "dp")

    weights = jnp.concatenate([w_gate[0], w_up[0], w_down[0].T], axis=0)
    weights = jnp.stack([weights[:, i * share : (i + 1) * share] for i in range(SIDE)])
    me = lax.axis_index("x")
    weights = jnp.stack(
        [
            lax.ppermute(take(weights, me + i), "x", [(d, (d + i) % SIDE) for d in range(SIDE)])
            if i
            else take(weights, me)
            for i in range(SIDE)
        ]
    )
    weights = [take(weights, me + SIDE - i) for i in range(SIDE)]
    held = [jnp.concatenate([w[i * feats : (i + 1) * feats] for w in weights], axis=0) for i in range(3)]

    q = jnp.arange(quarter * pieces, dtype=jnp.int32)
    q_place = (q % pieces) // CAP * block + q // pieces * CAP + q % CAP
    order = (q_place[None, :] == q[:, None]).astype(BF16)
    longer = pieces + 2
    p = jnp.arange(quarter * longer, dtype=jnp.int32)
    p_row = p % longer
    p_place = jnp.where(
        p_row < pieces, p_row // CAP * block + p // longer * CAP + p_row % CAP, p_row * quarter + p // longer
    )
    back_order = (p_place[:, None] == p[None, :]).astype(BF16)
    first_lanes = [(jnp.arange(LANES)[None, :] == i).astype(BF16) for i in range(2)]
    recv = recv.reshape(SIDE, quarter * pieces, LANES)
    recv = lax.dot_general(order, recv, (((1,), (1,)), ((), ())), preferred_element_type=BF16)
    recv = recv.reshape(2 * halves, block, SIDE, LANES).transpose(2, 1, 0, 3).reshape(slots, 2 * feats)
    recv, back_order, first_lanes, held = lax.optimization_barrier((recv, back_order, first_lanes, held))
    recv = exchange(jnp.broadcast_to(recv[None], (SIDE, slots, 2 * feats)), "x")
    tok = jnp.concatenate([recv[i, :, :feats] for i in range(SIDE)], axis=1)
    grad = jnp.concatenate([recv[i, :, feats:] for i in range(SIDE)], axis=1)
    pre = [times(v, w).astype(BF16) for v, w in zip((tok, tok, grad), held)]
    pre = jnp.concatenate(pre, axis=1)

    pre = exchange(pre.reshape(SIDE, slots // SIDE, 3 * share), "y")
    pre = jnp.sum(pre.astype(F32), axis=0)
    gate_pre, up_pre, grad_hidden = pre[:, :share], pre[:, share : 2 * share], pre[:, 2 * share :]
    logistic = jax.nn.sigmoid(gate_pre)
    silu = gate_pre * logistic
    act = (silu * up_pre).astype(BF16)
    grad_gate = (grad_hidden * up_pre * (logistic * (1.0 + gate_pre * (1.0 - logistic)))).astype(BF16)
    grad_up = (grad_hidden * silu).astype(BF16)
    dots = jnp.sum(act.astype(F32) * grad_hidden, axis=1, keepdims=True)
    dots = sum(v * lane for v, lane in zip(split2(dots), first_lanes))
    every = lax.all_gather(jnp.concatenate([act, grad_gate, grad_up, dots], axis=1), "y", axis=0, tiled=True)

    act, grad_gate, grad_up = (every[:, i * share : (i + 1) * share] for i in range(3))
    expert_out = times_t(act, held[2]).astype(BF16)
    grad_pick = (times_t(grad_gate, held[0]) + times_t(grad_up, held[1])).astype(BF16)
    dots = every[:, 3 * share].astype(F32) + every[:, 3 * share + 1].astype(F32)
    dots = jnp.pad(jnp.stack(split2(dots)), ((0, 6), (0, 2 * feats - slots)))
    back = jnp.stack(
        [
            jnp.concatenate(
                [
                    jnp.concatenate([v[:, i * feats : (i + 1) * feats] for v in (expert_out, grad_pick)], axis=1),
                    dots,
                ],
                axis=0,
            )
            for i in range(SIDE)
        ]
    )
    back = jnp.sum(exchange(back, "x").astype(F32), axis=0)
    dots = (back[slots, :slots] + back[slots + 1, :slots]).reshape(experts, CAP)
    dots = jnp.pad(dots, ((0, 0), (0, LANES - CAP))).reshape(SIDE, quarter, LANES)
    back = back[:slots].astype(BF16).reshape(SIDE, block, 2 * halves, LANES).transpose(0, 2, 1, 3)
    back = jnp.concatenate([back.reshape(SIDE, quarter * pieces, LANES), *split2(dots)], axis=1)

    back = lax.dot_general(back_order, back, (((1,), (1,)), ((), ())), preferred_element_type=BF16)
    back = back.transpose(1, 0, 2).reshape(experts, longer // 2, 2, LANES)
    back, rank, gate = lax.optimization_barrier((back, rank, gate))
    back = exchange(back, "dp").reshape(experts * longer, LANES)

    kinds = [g for g in split3(gate)] + [jnp.ones_like(gate)]
    value = jnp.concatenate([g for g in kinds for _ in range(halves)], axis=1)[:, None, :]
    mix = rows_of(rank, [i // 3 * halves + h for i in range(4) for h in range(halves)])
    all_rows = jnp.arange(longer, dtype=jnp.int32).astype(F32)[None, :, None]
    mix = jnp.where(mix == all_rows, value, 0.0).astype(BF16).reshape(experts * longer, -1)
    place = jnp.arange(experts * longer, dtype=jnp.int32)[None, :]
    last = (place // longer == jnp.arange(experts)[:, None]) & (place % longer >= pieces)
    back, mix, last = lax.optimization_barrier((back, mix, last.astype(BF16)))

    dots = times(last, back)
    dots = sum(jnp.where(rank == i, dots[:, i : i + 1], 0.0) for i in range(CAP))
    grad_gates = (jnp.sum(jnp.where(names, dots[None], 0.0), axis=1) / gates.T).T

    out = lax.dot_general(
        mix, back, (((0,), (0,)), ((), ())), preferred_element_type=F32
    ).reshape(4, halves, rows, LANES)
    mixed = out[0] + out[1] + out[2]
    mixed = jnp.concatenate([mixed[h] for h in range(halves)], axis=1).astype(BF16)
    grad_tokens = jnp.concatenate([out[3, h] for h in range(halves)], axis=1).astype(BF16)
    return mixed, grad_tokens, grad_gates


def solution(mesh):
    wide = Mesh(mesh.devices.reshape(mesh.devices.shape[0], SIDE, SIDE), ("dp", "y", "x"))
    split = ("y", "x")
    placed = (
        P("dp", split),
        P("dp", None),
        P("dp", None),
        P("dp", split, None),
        P("dp", split, None),
        P("dp", None, split),
        P("dp", split),
    )
    return jax.shard_map(
        shards,
        mesh=wide,
        in_specs=placed,
        out_specs=(P("dp", split), P("dp", split), P("dp", None)),
        check_vma=False,
    )
```

```python
import jax
import jax.numpy as jnp
from jax import lax
from jax.sharding import Mesh, PartitionSpec as P

CAP = 6
LANES = 128
SIDE = 4
F32 = jnp.float32
BF16 = jnp.bfloat16


def split3(v):
    hi = v.astype(BF16).astype(F32)
    mid = (v - hi).astype(BF16).astype(F32)
    return hi, mid, v - hi - mid


def exchange(v, axes):
    return lax.all_to_all(v, axes, split_axis=0, concat_axis=0, tiled=True)


def take(v, i):
    return lax.dynamic_index_in_dim(v, i % SIDE, axis=0, keepdims=False)


def routing(picks_t, gates_t, experts):
    ids = jnp.arange(experts, dtype=jnp.int32)
    names = picks_t[:, None, :] == ids[None, :, None]
    member = jnp.any(names, axis=0)
    gate = jnp.sum(jnp.where(names, gates_t[:, None, :], 0.0), axis=0)
    rows = picks_t.shape[1]
    before = jnp.arange(rows)[:, None] < jnp.arange(rows)[None, :]
    rank = jnp.dot(member.astype(BF16), before.astype(BF16), preferred_element_type=F32)
    return names, jnp.where(member, rank, -1000.0), gate


def split2(v):
    hi = v.astype(BF16)
    return hi, (v - hi.astype(F32)).astype(BF16)


def times(a, b):
    return jnp.dot(a, b, preferred_element_type=F32)


def times_t(a, b):
    return lax.dot_general(a, b, (((1,), (1,)), ((), ())), preferred_element_type=F32)


def shards(tokens, picks, gates, w_gate, w_up, w_down, cotangent):
    rows, feats = tokens.shape
    experts = lax.axis_size("dp")
    halves = feats // LANES
    pieces = 2 * halves * CAP
    hidden = w_gate.shape[2]
    quarter = experts // SIDE
    slots = experts * CAP
    block = quarter * CAP
    share = hidden // SIDE

    names, rank, gate = routing(picks.T, gates.T, experts)

    j = jnp.arange(pieces, dtype=jnp.int32)
    j_row = j.astype(F32)[None, :, None]

    def rows_of(rank, blocks):
        return jnp.concatenate([rank + CAP * i for i in blocks], axis=1)[:, None, :]

    source = jnp.concatenate(
        [v[:, h * LANES : (h + 1) * LANES] for v in (tokens, cotangent) for h in range(halves)], axis=0
    )

    def select(target, rows_from):
        mask = (target == j_row).astype(BF16).reshape(experts * pieces, -1)
        return times(mask, rows_from).reshape(experts, pieces, LANES)

    hit = rank[:, None, :] == (j % CAP).astype(F32)[None, :, None]
    scale = jnp.sum(jnp.where(hit, gate[:, None, :], 0.0), axis=2, keepdims=True)
    scale = jnp.where((j >= halves * CAP)[None, :, None], scale, 1.0)
    packed = (select(rows_of(rank, range(2 * halves)), source) * scale).astype(BF16)

    recv = exchange(packed, "dp")

    weights = jnp.concatenate([w_gate[0], w_up[0], w_down[0].T], axis=0)
    weights = jnp.stack([weights[:, i * share : (i + 1) * share] for i in range(SIDE)])
    me = lax.axis_index("x")
    weights = jnp.stack(
        [
            lax.ppermute(take(weights, me + i), "x", [(d, (d + i) % SIDE) for d in range(SIDE)])
            if i
            else take(weights, me)
            for i in range(SIDE)
        ]
    )
    weights = [take(weights, me + SIDE - i) for i in range(SIDE)]
    held = [jnp.concatenate([w[i * feats : (i + 1) * feats] for w in weights], axis=0) for i in range(3)]

    q = jnp.arange(quarter * pieces, dtype=jnp.int32)
    q_place = (q % pieces) // CAP * block + q // pieces * CAP + q % CAP
    order = (q_place[None, :] == q[:, None]).astype(BF16)
    longer = pieces + 2
    p = jnp.arange(quarter * longer, dtype=jnp.int32)
    p_row = p % longer
    p_place = jnp.where(
        p_row < pieces, p_row // CAP * block + p // longer * CAP + p_row % CAP, p_row * quarter + p // longer
    )
    back_order = (p_place[:, None] == p[None, :]).astype(BF16)
    place = jnp.arange(experts * longer, dtype=jnp.int32)[:, None]
    first_lanes = [(jnp.arange(LANES)[None, :] == i).astype(BF16) for i in range(2)]
    recv = recv.reshape(SIDE, quarter * pieces, LANES)
    recv = lax.dot_general(order, recv, (((1,), (1,)), ((), ())), preferred_element_type=BF16)
    recv = recv.reshape(2 * halves, block, SIDE, LANES).transpose(2, 1, 0, 3).reshape(slots, 2 * feats)
    recv, back_order, place, first_lanes, held = lax.optimization_barrier((recv, back_order, place, first_lanes, held))
    recv = exchange(jnp.broadcast_to(recv[None], (SIDE, slots, 2 * feats)), "x")
    tok = jnp.concatenate([recv[i, :, :feats] for i in range(SIDE)], axis=1)
    grad = jnp.concatenate([recv[i, :, feats:] for i in range(SIDE)], axis=1)
    pre = [times(v, w).astype(BF16) for v, w in zip((tok, tok, grad), held)]
    pre = jnp.concatenate(pre, axis=1)

    pre = exchange(pre.reshape(SIDE, slots // SIDE, 3 * share), "y")
    pre = jnp.sum(pre.astype(F32), axis=0)
    gate_pre, up_pre, grad_hidden = pre[:, :share], pre[:, share : 2 * share], pre[:, 2 * share :]
    logistic = jax.nn.sigmoid(gate_pre)
    silu = gate_pre * logistic
    act = (silu * up_pre).astype(BF16)
    grad_gate = (grad_hidden * up_pre * (logistic * (1.0 + gate_pre * (1.0 - logistic)))).astype(BF16)
    grad_up = (grad_hidden * silu).astype(BF16)
    dots = jnp.sum(act.astype(F32) * grad_hidden, axis=1, keepdims=True)
    dots = sum(v * lane for v, lane in zip(split2(dots), first_lanes))
    every = lax.all_gather(jnp.concatenate([act, grad_gate, grad_up, dots], axis=1), "y", axis=0, tiled=True)

    act, grad_gate, grad_up = (every[:, i * share : (i + 1) * share] for i in range(3))
    expert_out = times_t(act, held[2]).astype(BF16)
    grad_pick = (times_t(grad_gate, held[0]) + times_t(grad_up, held[1])).astype(BF16)
    dots = every[:, 3 * share].astype(F32) + every[:, 3 * share + 1].astype(F32)
    dots = jnp.pad(jnp.stack(split2(dots)), ((0, 6), (0, 2 * feats - slots)))
    back = jnp.stack(
        [
            jnp.concatenate(
                [
                    jnp.concatenate([v[:, i * feats : (i + 1) * feats] for v in (expert_out, grad_pick)], axis=1),
                    dots,
                ],
                axis=0,
            )
            for i in range(SIDE)
        ]
    )
    back = jnp.sum(exchange(back, "x").astype(F32), axis=0)
    dots = (back[slots, :slots] + back[slots + 1, :slots]).reshape(experts, CAP)
    dots = jnp.pad(dots, ((0, 0), (0, LANES - CAP))).reshape(SIDE, quarter, LANES)
    back = back[:slots].astype(BF16).reshape(SIDE, block, 2 * halves, LANES).transpose(0, 2, 1, 3)
    back = jnp.concatenate([back.reshape(SIDE, quarter * pieces, LANES), *split2(dots)], axis=1)

    back = lax.dot_general(back_order, back, (((1,), (1,)), ((), ())), preferred_element_type=BF16)
    back = back.transpose(1, 0, 2).reshape(experts, longer // 2, 2, LANES)
    back, rank, gate, place = lax.optimization_barrier((back, rank, gate, place))
    back = exchange(back, "dp").reshape(experts * longer, LANES)

    kinds = [g for g in split3(gate)] + [jnp.ones_like(gate)]
    value = jnp.concatenate([g for g in kinds for _ in range(halves)], axis=1).astype(BF16)
    target = jnp.concatenate([rank + CAP * (i // 3 * halves + h) for i in range(4) for h in range(halves)], axis=1)
    source_of = place // longer == jnp.arange(experts, dtype=jnp.int32)[None, :]
    spread = source_of.astype(BF16)
    mix = times(spread, target.astype(BF16)) == (place % longer).astype(F32)
    mix = jnp.where(mix, times(spread, value), 0.0).astype(BF16)
    last = (source_of & (place % longer >= pieces)).astype(BF16)
    mix = jnp.concatenate([mix, last], axis=1)
    back, mix = lax.optimization_barrier((back, mix))
    out = lax.dot_general(mix, back, (((0,), (0,)), ((), ())), preferred_element_type=F32)

    dots = out[4 * halves * rows :]
    dots = sum(jnp.where(rank == i, dots[:, i : i + 1], 0.0) for i in range(CAP))
    grad_gates = (jnp.sum(jnp.where(names, dots[None], 0.0), axis=1) / gates.T).T

    out = out[: 4 * halves * rows].reshape(4, halves, rows, LANES)
    mixed = out[0] + out[1] + out[2]
    mixed = jnp.concatenate([mixed[h] for h in range(halves)], axis=1).astype(BF16)
    grad_tokens = jnp.concatenate([out[3, h] for h in range(halves)], axis=1).astype(BF16)
    return mixed, grad_tokens, grad_gates


def solution(mesh):
    wide = Mesh(mesh.devices.reshape(mesh.devices.shape[0], SIDE, SIDE), ("dp", "y", "x"))
    split = ("y", "x")
    placed = (
        P("dp", split),
        P("dp", None),
        P("dp", None),
        P("dp", split, None),
        P("dp", split, None),
        P("dp", None, split),
        P("dp", split),
    )
    return jax.shard_map(
        shards,
        mesh=wide,
        in_specs=placed,
        out_specs=(P("dp", split), P("dp", split), P("dp", None)),
        check_vma=False,
    )
```

```python
import jax
import jax.numpy as jnp
from jax import lax
from jax.sharding import Mesh, PartitionSpec as P

CAP = 6
LANES = 128
SIDE = 4
F32 = jnp.float32
BF16 = jnp.bfloat16


def split3(v):
    hi = v.astype(BF16).astype(F32)
    mid = (v - hi).astype(BF16).astype(F32)
    return hi, mid, v - hi - mid


def exchange(v, axes):
    return lax.all_to_all(v, axes, split_axis=0, concat_axis=0, tiled=True)


def take(v, i):
    return lax.dynamic_index_in_dim(v, i % SIDE, axis=0, keepdims=False)


def routing(picks_t, gates_t, experts):
    ids = jnp.arange(experts, dtype=jnp.int32)
    names = picks_t[:, None, :] == ids[None, :, None]
    member = jnp.any(names, axis=0)
    gate = jnp.sum(jnp.where(names, gates_t[:, None, :], 0.0), axis=0)
    rows = picks_t.shape[1]
    before = jnp.arange(rows)[:, None] < jnp.arange(rows)[None, :]
    rank = jnp.dot(member.astype(BF16), before.astype(BF16), preferred_element_type=F32)
    return names, jnp.where(member, rank, -1000.0), gate


def split2(v):
    hi = v.astype(BF16)
    return hi, (v - hi.astype(F32)).astype(BF16)


def times(a, b):
    return jnp.dot(a, b, preferred_element_type=F32)


def times_t(a, b):
    return lax.dot_general(a, b, (((1,), (1,)), ((), ())), preferred_element_type=F32)


def shards(tokens, picks, gates, w_gate, w_up, w_down, cotangent):
    rows, feats = tokens.shape
    experts = lax.axis_size("dp")
    halves = feats // LANES
    pieces = 2 * halves * CAP
    hidden = w_gate.shape[2]
    quarter = experts // SIDE
    slots = experts * CAP
    block = quarter * CAP
    share = hidden // SIDE

    names, rank, gate = routing(picks.T, gates.T, experts)

    j = jnp.arange(pieces, dtype=jnp.int32)
    j_row = j.astype(F32)[None, :, None]

    def rows_of(rank, blocks):
        return jnp.concatenate([rank + CAP * i for i in blocks], axis=1)[:, None, :]

    source = jnp.concatenate(
        [v[:, h * LANES : (h + 1) * LANES] for v in (tokens, cotangent) for h in range(halves)], axis=0
    )

    def select(target, rows_from):
        mask = (target == j_row).astype(BF16).reshape(experts * pieces, -1)
        return times(mask, rows_from).reshape(experts, pieces, LANES)

    hit = rank[:, None, :] == (j % CAP).astype(F32)[None, :, None]
    scale = jnp.sum(jnp.where(hit, gate[:, None, :], 0.0), axis=2, keepdims=True)
    scale = jnp.where((j >= halves * CAP)[None, :, None], scale, 1.0)
    packed = (select(rows_of(rank, range(2 * halves)), source) * scale).astype(BF16)

    recv = exchange(packed, "dp")

    weights = jnp.concatenate([w_gate[0], w_up[0], w_down[0].T], axis=0)
    weights = jnp.stack([weights[:, i * share : (i + 1) * share] for i in range(SIDE)])
    me = lax.axis_index("x")
    came = [
        lax.ppermute(take(weights, me + i), "x", [(d, (d + i) % SIDE) for d in range(SIDE)])
        if i
        else take(weights, me)
        for i in range(SIDE)
    ]

    q = jnp.arange(quarter * pieces, dtype=jnp.int32)
    q_place = (q % pieces) // CAP * block + q // pieces * CAP + q % CAP
    order = (q_place[None, :] == q[:, None]).astype(BF16)
    longer = pieces + 2
    p = jnp.arange(quarter * longer, dtype=jnp.int32)
    p_row = p % longer
    p_place = jnp.where(
        p_row < pieces, p_row // CAP * block + p // longer * CAP + p_row % CAP, p_row * quarter + p // longer
    )
    back_order = (p_place[:, None] == p[None, :]).astype(BF16)
    place = jnp.arange(experts * longer, dtype=jnp.int32)[:, None]
    first_lanes = [(jnp.arange(LANES)[None, :] == i).astype(BF16) for i in range(2)]
    recv = recv.reshape(SIDE, quarter * pieces, LANES)
    recv = lax.dot_general(order, recv, (((1,), (1,)), ((), ())), preferred_element_type=BF16)
    recv = recv.reshape(2 * halves, block, SIDE, LANES).transpose(2, 1, 0, 3).reshape(slots, 2 * feats)
    recv, *came = lax.optimization_barrier((recv, *came))
    weights = jnp.stack(came)
    weights = [take(weights, me + SIDE - i) for i in range(SIDE)]
    held = [jnp.concatenate([w[i * feats : (i + 1) * feats] for w in weights], axis=0) for i in range(3)]
    recv, back_order, place, first_lanes, held = lax.optimization_barrier((recv, back_order, place, first_lanes, held))
    recv = exchange(jnp.broadcast_to(recv[None], (SIDE, slots, 2 * feats)), "x")
    tok = jnp.concatenate([recv[i, :, :feats] for i in range(SIDE)], axis=1)
    grad = jnp.concatenate([recv[i, :, feats:] for i in range(SIDE)], axis=1)
    pre = [times(v, w).astype(BF16) for v, w in zip((tok, tok, grad), held)]
    pre = jnp.concatenate(pre, axis=1)

    pre = exchange(pre.reshape(SIDE, slots // SIDE, 3 * share), "y")
    pre = jnp.sum(pre.astype(F32), axis=0)
    gate_pre, up_pre, grad_hidden = pre[:, :share], pre[:, share : 2 * share], pre[:, 2 * share :]
    logistic = jax.nn.sigmoid(gate_pre)
    silu = gate_pre * logistic
    act = (silu * up_pre).astype(BF16)
    grad_gate = (grad_hidden * up_pre * (logistic * (1.0 + gate_pre * (1.0 - logistic)))).astype(BF16)
    grad_up = (grad_hidden * silu).astype(BF16)
    dots = jnp.sum(act.astype(F32) * grad_hidden, axis=1, keepdims=True)
    dots = sum(v * lane for v, lane in zip(split2(dots), first_lanes))
    every = lax.all_gather(jnp.concatenate([act, grad_gate, grad_up, dots], axis=1), "y", axis=0, tiled=True)

    act, grad_gate, grad_up = (every[:, i * share : (i + 1) * share] for i in range(3))
    expert_out = times_t(act, held[2]).astype(BF16)
    grad_pick = (times_t(grad_gate, held[0]) + times_t(grad_up, held[1])).astype(BF16)
    dots = every[:, 3 * share].astype(F32) + every[:, 3 * share + 1].astype(F32)
    dots = jnp.pad(jnp.stack(split2(dots)), ((0, 6), (0, 2 * feats - slots)))
    back = jnp.stack(
        [
            jnp.concatenate(
                [
                    jnp.concatenate([v[:, i * feats : (i + 1) * feats] for v in (expert_out, grad_pick)], axis=1),
                    dots,
                ],
                axis=0,
            )
            for i in range(SIDE)
        ]
    )
    back = jnp.sum(exchange(back, "x").astype(F32), axis=0)
    dots = (back[slots, :slots] + back[slots + 1, :slots]).reshape(experts, CAP)
    dots = jnp.pad(dots, ((0, 0), (0, LANES - CAP))).reshape(SIDE, quarter, LANES)
    back = back[:slots].astype(BF16).reshape(SIDE, block, 2 * halves, LANES).transpose(0, 2, 1, 3)
    back = jnp.concatenate([back.reshape(SIDE, quarter * pieces, LANES), *split2(dots)], axis=1)

    back = lax.dot_general(back_order, back, (((1,), (1,)), ((), ())), preferred_element_type=BF16)
    back = back.transpose(1, 0, 2).reshape(experts, longer // 2, 2, LANES)
    back, rank, gate, place = lax.optimization_barrier((back, rank, gate, place))
    back = exchange(back, "dp").reshape(experts * longer, LANES)

    kinds = [g for g in split3(gate)] + [jnp.ones_like(gate)]
    value = jnp.concatenate([g for g in kinds for _ in range(halves)], axis=1).astype(BF16)
    target = jnp.concatenate([rank + CAP * (i // 3 * halves + h) for i in range(4) for h in range(halves)], axis=1)
    source_of = place // longer == jnp.arange(experts, dtype=jnp.int32)[None, :]
    spread = source_of.astype(BF16)
    mix = times(spread, target.astype(BF16)) == (place % longer).astype(F32)
    mix = jnp.where(mix, times(spread, value), 0.0).astype(BF16)
    last = (source_of & (place % longer >= pieces)).astype(BF16)
    mix = jnp.concatenate([mix, last], axis=1)
    back, mix = lax.optimization_barrier((back, mix))
    out = lax.dot_general(mix, back, (((0,), (0,)), ((), ())), preferred_element_type=F32)

    dots = out[4 * halves * rows :]
    dots = sum(jnp.where(rank == i, dots[:, i : i + 1], 0.0) for i in range(CAP))
    grad_gates = (jnp.sum(jnp.where(names, dots[None], 0.0), axis=1) / gates.T).T

    out = out[: 4 * halves * rows].reshape(4, halves, rows, LANES)
    mixed = out[0] + out[1] + out[2]
    mixed = jnp.concatenate([mixed[h] for h in range(halves)], axis=1).astype(BF16)
    grad_tokens = jnp.concatenate([out[3, h] for h in range(halves)], axis=1).astype(BF16)
    return mixed, grad_tokens, grad_gates


def solution(mesh):
    wide = Mesh(mesh.devices.reshape(mesh.devices.shape[0], SIDE, SIDE), ("dp", "y", "x"))
    split = ("y", "x")
    placed = (
        P("dp", split),
        P("dp", None),
        P("dp", None),
        P("dp", split, None),
        P("dp", split, None),
        P("dp", None, split),
        P("dp", split),
    )
    return jax.shard_map(
        shards,
        mesh=wide,
        in_specs=placed,
        out_specs=(P("dp", split), P("dp", split), P("dp", None)),
        check_vma=False,
    )
```

```python
import jax
import jax.numpy as jnp
from jax import lax
from jax.sharding import Mesh, PartitionSpec as P

CAP = 6
LANES = 128
SIDE = 4
F32 = jnp.float32
BF16 = jnp.bfloat16


def split3(v):
    hi = v.astype(BF16).astype(F32)
    mid = (v - hi).astype(BF16).astype(F32)
    return hi, mid, v - hi - mid


def exchange(v, axes):
    return lax.all_to_all(v, axes, split_axis=0, concat_axis=0, tiled=True)


def take(v, i):
    return lax.dynamic_index_in_dim(v, i % SIDE, axis=0, keepdims=False)


def routing(picks_t, gates_t, experts):
    ids = jnp.arange(experts, dtype=jnp.int32)
    names = picks_t[:, None, :] == ids[None, :, None]
    member = jnp.any(names, axis=0)
    gate = jnp.sum(jnp.where(names, gates_t[:, None, :], 0.0), axis=0)
    rows = picks_t.shape[1]
    before = jnp.arange(rows)[:, None] < jnp.arange(rows)[None, :]
    rank = jnp.dot(member.astype(BF16), before.astype(BF16), preferred_element_type=F32)
    return names, jnp.where(member, rank, -1000.0), gate


def split2(v):
    hi = v.astype(BF16)
    return hi, (v - hi.astype(F32)).astype(BF16)


def times(a, b):
    return jnp.dot(a, b, preferred_element_type=F32)


def times_t(a, b):
    return lax.dot_general(a, b, (((1,), (1,)), ((), ())), preferred_element_type=F32)


def shards(tokens, picks, gates, w_gate, w_up, w_down, cotangent):
    rows, feats = tokens.shape
    experts = lax.axis_size("dp")
    halves = feats // LANES
    pieces = 2 * halves * CAP
    hidden = w_gate.shape[2]
    quarter = experts // SIDE
    slots = experts * CAP
    block = quarter * CAP
    share = hidden // SIDE

    names, rank, gate = routing(picks.T, gates.T, experts)

    j = jnp.arange(pieces, dtype=jnp.int32)
    j_row = j.astype(F32)[None, :, None]

    def rows_of(rank, blocks):
        return jnp.concatenate([rank + CAP * i for i in blocks], axis=1)[:, None, :]

    source = jnp.concatenate(
        [v[:, h * LANES : (h + 1) * LANES] for v in (tokens, cotangent) for h in range(halves)], axis=0
    )

    def select(target, rows_from):
        mask = (target == j_row).astype(BF16).reshape(experts * pieces, -1)
        return times(mask, rows_from).reshape(experts, pieces, LANES)

    hit = rank[:, None, :] == (j % CAP).astype(F32)[None, :, None]
    scale = jnp.sum(jnp.where(hit, gate[:, None, :], 0.0), axis=2, keepdims=True)
    scale = jnp.where((j >= halves * CAP)[None, :, None], scale, 1.0)
    packed = (select(rows_of(rank, range(2 * halves)), source) * scale).astype(BF16)

    recv = exchange(packed, "dp")

    weights = jnp.concatenate([w_gate[0], w_up[0], w_down[0].T], axis=0)
    weights = jnp.stack([weights[:, i * share : (i + 1) * share] for i in range(SIDE)])
    me = lax.axis_index("x")
    came = [
        lax.ppermute(take(weights, me + i), "x", [(d, (d + i) % SIDE) for d in range(SIDE)])
        if i
        else take(weights, me)
        for i in range(SIDE)
    ]

    q = jnp.arange(quarter * pieces, dtype=jnp.int32)
    q_place = (q % pieces) // CAP * block + q // pieces * CAP + q % CAP
    order = (q_place[None, :] == q[:, None]).astype(BF16)
    longer = pieces + 2
    p = jnp.arange(quarter * longer, dtype=jnp.int32)
    p_row = p % longer
    p_place = jnp.where(
        p_row < pieces, p_row // CAP * block + p // longer * CAP + p_row % CAP, p_row * quarter + p // longer
    )
    back_order = (p_place[:, None] == p[None, :]).astype(BF16)
    place = jnp.arange(experts * longer, dtype=jnp.int32)[:, None]
    first_lanes = [(jnp.arange(LANES)[None, :] == i).astype(BF16) for i in range(2)]
    recv = recv.reshape(SIDE, quarter * pieces, LANES)
    recv = lax.dot_general(order, recv, (((1,), (1,)), ((), ())), preferred_element_type=BF16)
    recv = recv.reshape(2 * halves, block, SIDE, LANES).transpose(2, 1, 0, 3).reshape(slots, 2 * feats)
    recv, *came = lax.optimization_barrier((recv, *came))
    weights = jnp.stack(came)
    weights = [take(weights, me + SIDE - i) for i in range(SIDE)]
    held = [jnp.concatenate([w[i * feats : (i + 1) * feats] for w in weights], axis=0) for i in range(3)]
    held = [jnp.concatenate(held[:2], axis=1), held[2]]
    recv, back_order, place, first_lanes, held = lax.optimization_barrier((recv, back_order, place, first_lanes, held))
    recv = exchange(jnp.broadcast_to(recv[None], (SIDE, slots, 2 * feats)), "x")
    tok = jnp.concatenate([recv[i, :, :feats] for i in range(SIDE)], axis=1)
    grad = jnp.concatenate([recv[i, :, feats:] for i in range(SIDE)], axis=1)
    pre = [times(v, w).astype(BF16) for v, w in zip((tok, grad), held)]
    pre = jnp.concatenate(pre, axis=1)

    pre = exchange(pre.reshape(SIDE, slots // SIDE, 3 * share), "y")
    pre = jnp.sum(pre.astype(F32), axis=0)
    gate_pre, up_pre, grad_hidden = pre[:, :share], pre[:, share : 2 * share], pre[:, 2 * share :]
    logistic = jax.nn.sigmoid(gate_pre)
    silu = gate_pre * logistic
    act = (silu * up_pre).astype(BF16)
    grad_gate = (grad_hidden * up_pre * (logistic * (1.0 + gate_pre * (1.0 - logistic)))).astype(BF16)
    grad_up = (grad_hidden * silu).astype(BF16)
    dots = jnp.sum(act.astype(F32) * grad_hidden, axis=1, keepdims=True)
    dots = sum(v * lane for v, lane in zip(split2(dots), first_lanes))
    every = lax.all_gather(jnp.concatenate([act, grad_gate, grad_up, dots], axis=1), "y", axis=0, tiled=True)

    expert_out = times_t(every[:, :share], held[1]).astype(BF16)
    grad_pick = times_t(every[:, share : 3 * share], held[0]).astype(BF16)
    dots = every[:, 3 * share].astype(F32) + every[:, 3 * share + 1].astype(F32)
    dots = jnp.pad(jnp.stack(split2(dots)), ((0, 6), (0, 2 * feats - slots)))
    back = jnp.stack(
        [
            jnp.concatenate(
                [
                    jnp.concatenate([v[:, i * feats : (i + 1) * feats] for v in (expert_out, grad_pick)], axis=1),
                    dots,
                ],
                axis=0,
            )
            for i in range(SIDE)
        ]
    )
    back = jnp.sum(exchange(back, "x").astype(F32), axis=0)
    dots = (back[slots, :slots] + back[slots + 1, :slots]).reshape(experts, CAP)
    dots = jnp.pad(dots, ((0, 0), (0, LANES - CAP))).reshape(SIDE, quarter, LANES)
    back = back[:slots].astype(BF16).reshape(SIDE, block, 2 * halves, LANES).transpose(0, 2, 1, 3)
    back = jnp.concatenate([back.reshape(SIDE, quarter * pieces, LANES), *split2(dots)], axis=1)

    back = lax.dot_general(back_order, back, (((1,), (1,)), ((), ())), preferred_element_type=BF16)
    back = back.transpose(1, 0, 2).reshape(experts, longer // 2, 2, LANES)
    back, rank, gate, place = lax.optimization_barrier((back, rank, gate, place))
    back = exchange(back, "dp").reshape(experts * longer, LANES)

    kinds = [g for g in split3(gate)] + [jnp.ones_like(gate)]
    value = jnp.concatenate([g for g in kinds for _ in range(halves)], axis=1).astype(BF16)
    target = jnp.concatenate([rank + CAP * (i // 3 * halves + h) for i in range(4) for h in range(halves)], axis=1)
    source_of = place // longer == jnp.arange(experts, dtype=jnp.int32)[None, :]
    spread = source_of.astype(BF16)
    mix = times(spread, target.astype(BF16)) == (place % longer).astype(F32)
    mix = jnp.where(mix, times(spread, value), 0.0).astype(BF16)
    last = (source_of & (place % longer >= pieces)).astype(BF16)
    mix = jnp.concatenate([mix, last], axis=1)
    back, mix = lax.optimization_barrier((back, mix))
    out = lax.dot_general(mix, back, (((0,), (0,)), ((), ())), preferred_element_type=F32)

    dots = out[4 * halves * rows :]
    dots = sum(jnp.where(rank == i, dots[:, i : i + 1], 0.0) for i in range(CAP))
    grad_gates = (jnp.sum(jnp.where(names, dots[None], 0.0), axis=1) / gates.T).T

    out = out[: 4 * halves * rows].reshape(4, halves, rows, LANES)
    mixed = out[0] + out[1] + out[2]
    mixed = jnp.concatenate([mixed[h] for h in range(halves)], axis=1).astype(BF16)
    grad_tokens = jnp.concatenate([out[3, h] for h in range(halves)], axis=1).astype(BF16)
    return mixed, grad_tokens, grad_gates


def solution(mesh):
    wide = Mesh(mesh.devices.reshape(mesh.devices.shape[0], SIDE, SIDE), ("dp", "y", "x"))
    split = ("y", "x")
    placed = (
        P("dp", split),
        P("dp", None),
        P("dp", None),
        P("dp", split, None),
        P("dp", split, None),
        P("dp", None, split),
        P("dp", split),
    )
    return jax.shard_map(
        shards,
        mesh=wide,
        in_specs=placed,
        out_specs=(P("dp", split), P("dp", split), P("dp", None)),
        check_vma=False,
    )
```
